512 devices in a mesh: dp: 32 (over z, y_lo), mp: 16 (over y_hi, x, core).
Axes of the slice: x: 4, y: 4 (y_hi: 2, y_lo: 2; y = y_hi * 2 + y_lo), z: 16, core: 2. Of those that a mesh axis runs over, the one named last changes fastest.
Arguments:
- grads: bfloat16 [32, 32, 512, 512], P('dp', 'mp'), may hold values from -3500 to 3500
- order: int32 [16, 4], P('mp'), may hold values from 0 to 3, each once within a row
- offset: int32 [16], P('mp'), may hold values from 0 to 3
- prev_roots: bfloat16 [64, 512, 512], P('mp'), may hold values from -0.1 to 1.5
Outputs:
- update: bfloat16 [32, 32, 512, 512], P('dp', 'mp')
The draws below stay inside these ranges and needn't reach their ends.
Inputs may be any that keep to these rules, and one draw needn't show every extreme that they name: `order`: each row holds every number of 0 to 3 once.
All inputs are finite; a program needn't handle non-finite values.
Results may differ from the reference program's by a relative error of at most 0.0019.
The reference program's roundings to bfloat16 on the way (of `fresh`, `roots` and `half_done`) count: a program that leaves them out, or rounds other values in their place, can miss the bound.
Values may be sent and summed in bfloat16 or wider, within the bound.
A program may use at most 64 MiB of HBM per device.

```python
import math
import jax
import jax.numpy as jnp
from jax import lax

BLOCK = 512
NBLK = 2
REFRESH = 2
ITERS = 3
ITEMS = 4
N_DP = 32
N_MP = 16


def draw_grads(key, part):
    key = jax.random.fold_in(key, 11)
    keys = jax.random.split(key, 3)
    shard_blocks = N_MP * NBLK
    shape = (N_DP, shard_blocks, BLOCK, BLOCK)
    ramp = 1.0 + 0.35 * jnp.arange(BLOCK, dtype=jnp.float32) / BLOCK
    row_scale = jnp.exp(jax.random.uniform(keys[1], (1, shard_blocks, BLOCK, 1)) * 0.5 * math.log(10.0)) * ramp[None, None, :, None]
    col_scale = jnp.exp(jax.random.uniform(keys[2], (1, shard_blocks, 1, BLOCK)) * 0.5 * math.log(10.0)) * ramp[None, None, None, :]
    replica = 1.0 + jnp.arange(N_DP, dtype=jnp.float32) / max(N_DP - 1, 1)
    column = 1.0 + (jnp.arange(shard_blocks) // NBLK).astype(jnp.float32) / max(N_MP - 1, 1)
    band_owner = jnp.arange(BLOCK, dtype=jnp.int32) // (BLOCK // N_DP)
    own_band = (band_owner[None, :] == jnp.arange(N_DP, dtype=jnp.int32)[:, None]).astype(jnp.float32)
    band_boost = 1.0 + 3.0 * own_band
    boost = band_boost[:, None, :, None] * band_boost[:, None, None, :]
    base = jnp.clip(jax.random.normal(keys[0], shape), -3.0, 3.0)
    values = base * row_scale * col_scale * replica[:, None, None, None] * column[None, :, None, None] * boost
    return values.astype(jnp.bfloat16)


def draw_prev_roots(key, part):
    key = jax.random.fold_in(key, 23)
    keys = jax.random.split(key, 2)
    count = N_MP * ITEMS
    diagonal = jnp.exp(jax.random.uniform(keys[0], (count, BLOCK, 1), minval=math.log(0.5), maxval=math.log(1.5)))
    noise = jax.random.uniform(keys[1], (count, BLOCK, BLOCK), minval=-1.0, maxval=1.0) * (0.3 * math.sqrt(3.0) / math.sqrt(BLOCK))
    mirrored = (noise + jnp.swapaxes(noise, 1, 2)) / math.sqrt(2.0)
    identity = jnp.eye(BLOCK, dtype=jnp.float32)[None]
    values = identity * diagonal + mirrored * (1.0 - identity)
    return values.astype(jnp.bfloat16)


def with_ends(entries, own_key, least, high):
    index_at = [jax.random.randint(jax.random.fold_in(own_key, axis), (), 0, length) for axis, length in enumerate(entries.shape)]
    widest = entries.shape.index(max(entries.shape))
    beside = index_at[:widest] + [(index_at[widest] + 1) % entries.shape[widest]] + index_at[widest + 1:]
    return entries.at[tuple(index_at)].set(least).at[tuple(beside)].set(high)


def setup_inputs(seed: int = 0) -> dict:
    key_of = jax.random.split(jax.random.key(seed), 5)
    return {
        "grads": draw_grads(jax.random.fold_in(key_of[4], 71), 0),
        "order": jax.vmap(lambda own: jax.random.permutation(own, ITEMS))(jax.random.split(key_of[1], N_MP)).reshape((N_MP, ITEMS)).astype(jnp.int32),
        "offset": with_ends(jax.random.randint(key_of[2], (N_MP,), 0, ITEMS), jax.random.fold_in(key_of[2], 1), 0, ITEMS - 1).astype(jnp.int32),
        "prev_roots": draw_prev_roots(jax.random.fold_in(key_of[4], 71), 0),
    }


ridge = 0.1

def product(first, second):
    return jnp.dot(first, second, precision=lax.Precision.HIGHEST)

def newton_root(statistic):
    identity = jnp.eye(BLOCK, dtype=jnp.float32)
    ridged = statistic / (BLOCK * N_DP) + ridge * identity
    start_scale = 2.5 / jnp.sqrt(jnp.sum(ridged * ridged))
    current = start_scale * ridged
    root_now = jnp.sqrt(jnp.sqrt(start_scale)) * identity
    for step_index in range(ITERS):
        factor = (5.0 * identity - current) * 0.25
        root_now = product(root_now, factor)
        if step_index < ITERS - 1:
            factor_sq = product(factor, factor)
            current = product(product(factor_sq, factor_sq), current)
    return root_now.astype(jnp.bfloat16)

def column_update(shard_index, grads, order, offset, prev_roots):
    columns = lax.dynamic_slice_in_dim(grads, shard_index * NBLK, NBLK, 1)
    slot_list = (offset[shard_index] + jnp.arange(REFRESH, dtype=jnp.int32)) % ITEMS
    chosen = order[shard_index][slot_list]

    def one_stat(item_index):
        replicas = columns[:, item_index // 2]

        def accumulate(carried, gradient):
            turned = jnp.where(item_index % 2 == 0, gradient, gradient.T)
            term = lax.dot_general(turned, turned, (((1,), (1,)), ((), ())), preferred_element_type=jnp.float32)
            return (carried + term, None)
        summed, unused = lax.scan(accumulate, jnp.zeros((BLOCK, BLOCK), jnp.float32), replicas)
        return newton_root(summed)
    fresh = lax.map(one_stat, chosen)
    roots = lax.dynamic_slice_in_dim(prev_roots, shard_index * ITEMS, ITEMS, 0).at[chosen].set(fresh)
    left_roots = roots[0::2].astype(jnp.float32)
    right_roots = roots[1::2].astype(jnp.float32)
    half_done = jnp.einsum('bij,dbjk->dbik', left_roots, columns.astype(jnp.float32)).astype(jnp.bfloat16)
    return jnp.einsum('dbij,bjk->dbik', half_done.astype(jnp.float32), right_roots)

def reference(grads, order, offset, prev_roots):
    shards = jnp.arange(N_MP, dtype=jnp.int32)
    unscaled = lax.map(lambda shard_index: column_update(shard_index, grads, order, offset, prev_roots), shards)
    unscaled = jnp.moveaxis(unscaled, 0, 1).reshape(N_DP, N_MP * NBLK, BLOCK, BLOCK)
    grad_float = grads.astype(jnp.float32)
    grad_sq = lax.optimization_barrier(jnp.sum(grad_float * grad_float, axis=(1, 2, 3)))
    pre_sq = lax.optimization_barrier(jnp.sum(unscaled * unscaled, axis=(1, 2, 3)))
    factor = jnp.sqrt(grad_sq / (pre_sq + 1e-06))
    return (unscaled * factor[:, None, None, None]).astype(jnp.bfloat16)
```

```python
import functools

import jax
import jax.numpy as jnp
from jax import lax
from jax.experimental import pallas as pl
from jax.experimental.pallas import tpu as pltpu
from jax.sharding import PartitionSpec as P

MESH = pl.DeviceIdType.MESH
N = 512
T = 128
REPLICAS = 32
RING = 16
PEERS = 16
RIDGE = 0.1
PAIRS = [(i, j) for i in range(N // T) for j in range(i, N // T)]
ROWS = len(PAIRS) * T
PARTS = 2
PART = ROWS // PARTS
MEMBERS = (1, 2, -1)
LEADERS = (4, -4, 8)


def part(index):
    return pl.ds(index * PART, PART)


def small(a, b):
    return jnp.dot(a.astype(jnp.bfloat16), b.astype(jnp.bfloat16), preferred_element_type=jnp.float32)


def upper(full):
    return [full[i * T:(i + 1) * T, j * T:(j + 1) * T] for i, j in PAIRS]


def unpack(packed_ref, full_ref, scale=None):
    for index, (i, j) in enumerate(PAIRS):
        block = packed_ref[index * T:(index + 1) * T, :]
        full_ref[i * T:(i + 1) * T, j * T:(j + 1) * T] = block
        if i != j:
            full_ref[j * T:(j + 1) * T, i * T:(i + 1) * T] = block.T


def next_state(a):
    e2 = (small(a, a) - 10.0 * a) * 0.0625
    e4 = 3.125 * e2 + small(e2, e2)
    return 2.44140625 * a + small(e4, a)


def inverse_root(stat):
    row = lax.broadcasted_iota(jnp.int32, (N, N), 0)
    column = lax.broadcasted_iota(jnp.int32, (N, N), 1)
    eye = jnp.where(row == column, 1.0, 0.0)
    ridged = stat * (1.0 / (N * REPLICAS)) + RIDGE * eye
    total = jnp.sum(jnp.sum(ridged * ridged, axis=0, keepdims=True), axis=1, keepdims=True)
    start = 2.5 / jnp.sqrt(total)
    a = start * ridged
    b = next_state(a)
    c = next_state(b)
    g = small(a, b) * 0.0625 - 0.3125 * (a + b)
    root = 1.953125 * eye + 1.25 * g - 0.390625 * c - 0.25 * small(g, c)
    return jnp.sqrt(jnp.sqrt(start)) * root


def kernel(order, offset, grads, prev, out, old, stat, mine, sent, near, far, across, fresh, full, work, half, norms,
           old_sem, near_send, near_recv, far_send, far_recv, across_send, across_recv, fresh_send, fresh_recv,
           norm_send, norm_recv):
    dp, mp = lax.axis_index("dp"), lax.axis_index("mp")
    z, core = dp // 2, mp % 2
    sign = 1 - 2 * core

    def along(step):
        return (lax.rem(dp + 2 * step + 2 * RING, 2 * RING), mp)

    beside = (dp + 1 - 2 * (dp % 2), mp)

    load_old = pltpu.make_async_copy(prev, old, old_sem)
    load_old.start()

    barrier = pltpu.get_barrier_semaphore()
    for step in (1, -1, 2, -2, 4, -4, 8):
        pl.semaphore_signal(barrier, inc=1, device_id=along(step), device_id_type=MESH)
    pl.semaphore_signal(barrier, inc=1, device_id=beside, device_id_type=MESH)

    def greet(k, unused):
        pl.semaphore_signal(barrier, inc=1, device_id=(dp, lax.rem(mp + k, PEERS)), device_id_type=MESH)
        return unused

    lax.fori_loop(1, PEERS, greet, 0)

    place = [lax.rem(sign * (z - 5 * (2 * slot + core)) + 8 * RING, RING) for slot in range(2)]
    role = [lax.rem(p, 4) for p in place]
    leads = jnp.logical_or(role[0] == 0, role[1] == 0)
    lead_slot = jnp.where(role[1] == 0, 1, 0)
    lead_place = jnp.where(role[1] == 0, place[1], place[0])
    is_root = jnp.logical_and(leads, lead_place == 0)
    is_leaf_leader = jnp.logical_and(leads, lead_place != 0)

    items = [order[0, (offset[0] + slot) % 4] for slot in range(2)]

    def send_near(slot, k, index):
        return pltpu.make_async_remote_copy(
            src_ref=sent.at[slot, part(index)], dst_ref=near.at[k, part(index)],
            send_sem=near_send.at[slot, index], recv_sem=near_recv.at[k, index],
            device_id=along(-sign * MEMBERS[k]), device_id_type=MESH)

    for slot in range(2):
        item = items[slot]
        picked = grads[0, item // 2]
        turned = jnp.where(item % 2 == 0, picked, picked.T)
        product = lax.dot_general(turned, turned, (((1,), (1,)), ((), ())), preferred_element_type=jnp.float32)
        for index, block in enumerate(upper(product)):
            stat[slot, index * T:(index + 1) * T, :] = block
            sent[slot, index * T:(index + 1) * T, :] = block.astype(jnp.bfloat16)
        if slot == 0:
            pl.semaphore_wait(barrier, 7 + 1 + PEERS - 1)
        for k in range(3):
            @pl.when(role[slot] == k + 1)
            def _():
                for index in range(PARTS):
                    send_near(slot, k, index).start()

    grad_sq = jnp.zeros((1, 1), jnp.float32)
    for b in range(2):
        value = grads[0, b].astype(jnp.float32)
        grad_sq += jnp.sum(jnp.sum(value * value, axis=0, keepdims=True), axis=1, keepdims=True)

    def send_far(k, index):
        return pltpu.make_async_remote_copy(
            src_ref=mine.at[part(index)], dst_ref=far.at[k, part(index)],
            send_sem=far_send.at[index], recv_sem=far_recv.at[k, index],
            device_id=along(-sign * LEADERS[k]), device_id_type=MESH)

    def send_across(index):
        return pltpu.make_async_remote_copy(
            src_ref=mine.at[part(index)], dst_ref=across.at[part(index)],
            send_sem=across_send.at[index], recv_sem=across_recv.at[index],
            device_id=beside, device_id_type=MESH)

    @pl.when(leads)
    def _():
        for index in range(PARTS):
            for k in range(3):
                send_near(0, k, index).wait_recv()
            total = stat[lead_slot, part(index)]
            for k in range(3):
                total += near[k, part(index)].astype(jnp.float32)
            work[part(index)] = total
            mine[part(index)] = total.astype(jnp.bfloat16)
            for k in range(3):
                @pl.when(lead_place == LEADERS[k] % RING)
                def _():
                    send_far(k, index).start()

    def send_fresh(slot, step, k, index):
        return pltpu.make_async_remote_copy(
            src_ref=fresh.at[slot, part(index)], dst_ref=fresh.at[slot, part(index)],
            send_sem=fresh_send.at[k, index], recv_sem=fresh_recv.at[slot, index],
            device_id=along(step), device_id_type=MESH)

    @pl.when(is_root)
    def _():
        for index in range(PARTS):
            for k in range(3):
                send_far(k, index).wait_recv()
            total = work[part(index)]
            for k in range(3):
                total += far[k, part(index)].astype(jnp.float32)
            work[part(index)] = total
            mine[part(index)] = total.astype(jnp.bfloat16)
            send_across(index).start()
        for index in range(PARTS):
            send_across(index).wait_recv()
            work[part(index)] += across[part(index)].astype(jnp.float32)
        unpack(work, full)
        root = inverse_root(full[...])
        for index, block in enumerate(upper(root)):
            fresh[lead_slot, index * T:(index + 1) * T, :] = block.astype(jnp.bfloat16)
        for index in range(PARTS):
            for k, step in enumerate(LEADERS + MEMBERS):
                send_fresh(lead_slot, sign * step, k, index).start()

    @pl.when(is_leaf_leader)
    def _():
        for index in range(PARTS):
            send_fresh(lead_slot, 1, 0, index).wait_recv()
            for k, step in enumerate(MEMBERS):
                send_fresh(lead_slot, sign * step, 3 + k, index).start()

    load_old.wait()
    for slot in range(2):
        @pl.when(role[slot] != 0)
        def _():
            for index in range(PARTS):
                send_fresh(slot, 1, 0, index).wait_recv()
        unpack(fresh.at[slot], half.at[slot])

    pre_sq = jnp.zeros((1, 1), jnp.float32)
    for b in range(2):
        pair = []
        for side in range(2):
            k = 2 * b + side
            pair.append(jnp.where(items[0] == k, half[0], jnp.where(items[1] == k, half[1], old[k])))
        done = jnp.dot(pair[0], grads[0, b], preferred_element_type=jnp.float32).astype(jnp.bfloat16)
        unscaled = jnp.dot(done, pair[1], preferred_element_type=jnp.float32)
        full2 = unscaled
        pre_sq += jnp.sum(jnp.sum(full2 * full2, axis=0, keepdims=True), axis=1, keepdims=True)
        if b == 0:
            full[...] = unscaled
        else:
            last = unscaled

    line = lax.broadcasted_iota(jnp.int32, (8, T), 0)
    norms[mp] = jnp.where(line == 0, grad_sq, pre_sq)

    def send_norm(k):
        return pltpu.make_async_remote_copy(
            src_ref=norms.at[mp], dst_ref=norms.at[mp], send_sem=norm_send.at[k], recv_sem=norm_recv.at[mp],
            device_id=(dp, lax.rem(mp + k, PEERS)), device_id_type=MESH)

    def recv_norm(k):
        source = lax.rem(mp + k, PEERS)
        return pltpu.make_async_remote_copy(
            src_ref=norms.at[source], dst_ref=norms.at[source], send_sem=norm_send.at[k], recv_sem=norm_recv.at[source],
            device_id=(dp, source), device_id_type=MESH)

    def start_norm(k, unused):
        send_norm(k).start()
        return unused

    def end_norm(k, unused):
        recv_norm(k).wait_recv()
        return unused

    def end_send(k, unused):
        send_norm(k).wait_send()
        return unused

    lax.fori_loop(1, PEERS, start_norm, 0)
    lax.fori_loop(1, PEERS, end_norm, 0)
    total = norms[0]
    for k in range(1, PEERS):
        total += norms[k]
    factor = jnp.sqrt(total[0:1, 0:1] / (total[1:2, 0:1] + 1e-06))
    out[0, 0] = (full[...] * factor).astype(jnp.bfloat16)
    out[0, 1] = (last * factor).astype(jnp.bfloat16)

    lax.fori_loop(1, PEERS, end_send, 0)
    for slot in range(2):
        @pl.when(role[slot] != 0)
        def _():
            for index in range(PARTS):
                send_near(slot, 0, index).wait_send()

    @pl.when(is_root)
    def _():
        for index in range(PARTS):
            send_across(index).wait_send()
            for k in range(3):
                send_fresh(lead_slot, 1, k, index).wait_send()

    @pl.when(is_leaf_leader)
    def _():
        for index in range(PARTS):
            send_far(0, index).wait_send()

    @pl.when(leads)
    def _():
        for index in range(PARTS):
            for k in range(3):
                send_fresh(lead_slot, 1, 3 + k, index).wait_send()


def body(grads, order, offset, prev_roots):
    bf16, f32 = jnp.bfloat16, jnp.float32
    dma = pltpu.SemaphoreType.DMA
    return pl.pallas_call(
        kernel,
        out_shape=jax.ShapeDtypeStruct((1, 2, N, N), bf16),
        in_specs=[
            pl.BlockSpec(memory_space=pltpu.SMEM),
            pl.BlockSpec(memory_space=pltpu.SMEM),
            pl.BlockSpec(memory_space=pltpu.VMEM),
            pl.BlockSpec(memory_space=pl.ANY),
        ],
        out_specs=pl.BlockSpec(memory_space=pltpu.VMEM),
        scratch_shapes=[
            pltpu.VMEM((4, N, N), bf16),
            pltpu.VMEM((2, ROWS, T), f32),
            pltpu.VMEM((ROWS, T), bf16),
            pltpu.VMEM((2, ROWS, T), bf16),
            pltpu.VMEM((3, ROWS, T), bf16),
            pltpu.VMEM((3, ROWS, T), bf16),
            pltpu.VMEM((ROWS, T), bf16),
            pltpu.VMEM((2, ROWS, T), bf16),
            pltpu.VMEM((N, N), f32),
            pltpu.VMEM((ROWS, T), f32),
            pltpu.VMEM((2, N, N), bf16),
            pltpu.VMEM((PEERS, 8, T), f32),
            dma,
            dma((2, PARTS)), dma((3, PARTS)),
            dma((PARTS,)), dma((3, PARTS)),
            dma((PARTS,)), dma((PARTS,)),
            dma((6, PARTS)), dma((2, PARTS)),
            dma((PEERS,)), dma((PEERS,)),
        ],
        compiler_params=pltpu.CompilerParams(
            collective_id=0, has_side_effects=True, vmem_limit_bytes=48 * 1024 * 1024),
        cost_estimate=pl.CostEstimate(flops=10 * 2 * N ** 3, bytes_accessed=4 * 1024 * 1024, transcendentals=0),
        name="refresh",
    )(order, offset, grads, prev_roots)


def solution(mesh):
    placed = (P("dp", "mp", None, None), P("mp", None), P("mp"), P("mp", None, None))
    return jax.shard_map(
        body, mesh=mesh, in_specs=placed, out_specs=P("dp", "mp", None, None), check_vma=False
    )
```

```python
import jax
import jax.numpy as jnp
from jax import lax
from jax.experimental import pallas as pl
from jax.experimental.pallas import tpu as pltpu
from jax.sharding import PartitionSpec as P

MESH = pl.DeviceIdType.MESH
N = 512
T = 128
REPLICAS = 32
RING = 16
PEERS = 16
RIDGE = 0.1
ABOVE = (((0, 1), (0, 2), (0, 3)), ((1, 2), (1, 3), (2, 3)))
HALF = 4 * T + 16
PARTS = ((0, 256), (256, 272))
MEMBERS = (1, 2, -1)
LEADERS = (4, -4, 8)
GREETED = 7 + 5 + PEERS - 1


def part(index):
    return pl.ds(*PARTS[index])


def small(a, b):
    return jnp.dot(a.astype(jnp.bfloat16), b.astype(jnp.bfloat16), preferred_element_type=jnp.float32)


def total_square(value):
    return jnp.sum(jnp.sum(value * value, axis=0, keepdims=True), axis=1, keepdims=True)


def positions(rows, columns):
    shape = (rows, columns)
    return lax.broadcasted_iota(jnp.int32, shape, 0), lax.broadcasted_iota(jnp.int32, shape, 1)


def pack(top, bottom, store):
    row, column = positions(T, T)
    for h in range(2):
        tile = lambda i, j: (top[i * T:(i + 1) * T, j * T:(j + 1) * T] if i < 2 else
                             bottom[(i - 2) * T:(i - 1) * T, (j - 2) * T:(j - 1) * T])
        first, second = tile(2 * h, 2 * h), tile(2 * h + 1, 2 * h + 1)
        store(h, 0, jnp.where(column >= row, first, second))
        for index, (i, j) in enumerate(ABOVE[h]):
            store(h, (index + 1) * T, tile(i, j))
        diagonal = jnp.sum(jnp.where(column == row, second, 0.0), axis=0, keepdims=True)
        store(h, 4 * T, jnp.broadcast_to(diagonal, (16, T)))


def unpack(packed, full):
    row, column = positions(T, T)
    for h in range(2):
        both = packed[h, 0:T, :].astype(jnp.float32)
        mirrored = both.T
        diagonal = packed[h, 4 * T:4 * T + 16, :].astype(jnp.float32)[0:1]
        first = jnp.where(column >= row, both, mirrored)
        second = jnp.where(column < row, both, jnp.where(column == row, diagonal, mirrored))
        for block, i in ((first, 2 * h), (second, 2 * h + 1)):
            full[i * T:(i + 1) * T, i * T:(i + 1) * T] = block.astype(full.dtype)
        for index, (i, j) in enumerate(ABOVE[h]):
            block = packed[h, (index + 1) * T:(index + 2) * T, :]
            full[i * T:(i + 1) * T, j * T:(j + 1) * T] = block
            full[j * T:(j + 1) * T, i * T:(i + 1) * T] = block.T


def next_state(a):
    e2 = (small(a, a) - 10.0 * a) * 0.0625
    e4 = 3.125 * e2 + small(e2, e2)
    return 2.44140625 * a + small(e4, a)


def inverse_root(stat):
    row, column = positions(N, N)
    eye = jnp.where(row == column, 1.0, 0.0)
    ridged = stat * (1.0 / (N * REPLICAS)) + RIDGE * eye
    start = 2.5 / jnp.sqrt(total_square(ridged))
    a = start * ridged
    b = next_state(a)
    c = next_state(b)
    g = small(a, b) * 0.0625 - 0.3125 * (a + b)
    scale = jnp.sqrt(jnp.sqrt(start))
    top, bottom = (
        scale * (1.953125 * eye[rows, columns] + 1.25 * g[rows, columns] - 0.390625 * c[rows, columns]
                 - 0.25 * small(g[rows], c[:, columns]))
        for rows, columns in ((slice(0, 256), slice(0, N)), (slice(256, N), slice(256, N))))
    return top, bottom


def kernel(order, offset, grads, prev, out, order_here, offset_here, own, old, stat, sent, near, mine, far, across, both, fresh,
           full, roots, norms, order_sem, offset_sem, own_sem, old_sem, near_send, near_recv, far_send, far_recv, across_send,
           across_recv, fresh_send, fresh_recv, norm_send, norm_recv):
    dp, mp = lax.axis_index("dp"), lax.axis_index("mp")
    z, line, core = dp // 2, dp % 2, mp % 2
    sign = 1 - 2 * core

    loads = [pltpu.make_async_copy(*refs) for refs in (
        (order, order_here, order_sem), (offset, offset_here, offset_sem), (grads, own, own_sem), (prev, old, old_sem))]
    for load in loads:
        load.start()

    def along(step, flip=False):
        there = lax.rem(dp + 2 * step + 2 * RING, 2 * RING)
        return (there + 1 - 2 * line if flip else there, mp)

    barrier = pltpu.get_barrier_semaphore()
    for step in (1, -1, 2, -2, 4, -4, 8):
        pl.semaphore_signal(barrier, inc=1, device_id=along(step), device_id_type=MESH)
    for step in (0, 1, -1, 2, -2):
        pl.semaphore_signal(barrier, inc=1, device_id=along(step, True), device_id_type=MESH)

    def greet(k, unused):
        pl.semaphore_signal(barrier, inc=1, device_id=(dp, lax.rem(mp + k, PEERS)), device_id_type=MESH)
        return unused

    lax.fori_loop(1, PEERS, greet, 0)

    place = [lax.rem(sign * (z - 5 * (2 * slot + core)) + 8 * RING, RING) for slot in range(2)]
    role = [lax.rem(p, 4) for p in place]
    leads = jnp.logical_or(role[0] == 0, role[1] == 0)
    lead_slot = jnp.where(role[1] == 0, 1, 0)
    lead_place = jnp.where(role[1] == 0, place[1], place[0])
    is_root = jnp.logical_and(leads, lead_place == 0)
    passes_on = jnp.logical_and(leads, lead_place != 0)

    def remote(source, target, send_sem, recv_sem, device):
        return pltpu.make_async_remote_copy(
            src_ref=source, dst_ref=target, send_sem=send_sem, recv_sem=recv_sem, device_id=device, device_id_type=MESH)

    def send_near(slot, k, index):
        half = line if k < 3 else 1 - line
        device = along(0 if k == 6 else -sign * MEMBERS[k % 3], k >= 3)
        return remote(sent.at[slot, half, part(index)], near.at[k, part(index)],
                      near_send.at[slot, 0 if k < 3 else 1, index], near_recv.at[k, index], device)

    def send_far(k, index):
        return remote(mine.at[part(index)], far.at[k, part(index)], far_send.at[index], far_recv.at[k, index],
                      along(-sign * LEADERS[k]))

    def send_across(index):
        return remote(mine.at[part(index)], across.at[part(index)], across_send.at[index], across_recv.at[index],
                      along(0, True))

    def send_fresh(slot, half, k, index):
        step = 0 if k == 9 else sign * (LEADERS + MEMBERS + MEMBERS)[k]
        return remote(fresh.at[slot, half, part(index)], fresh.at[slot, half, part(index)], fresh_send.at[k, index],
                      fresh_recv.at[slot, half, index], along(step, k >= 6))

    loads[0].wait()
    loads[1].wait()
    items = [order_here[0, (offset_here[0] + slot) % 4] for slot in range(2)]
    loads[2].wait()
    for slot in range(2):
        item = items[slot]
        picked = own[0, item // 2]
        turned = jnp.where(item % 2 == 0, picked, picked.T)
        top, bottom = (
            lax.dot_general(a, b, (((1,), (1,)), ((), ())), preferred_element_type=jnp.float32)
            for a, b in ((turned[:256], turned), (turned[256:], turned[256:])))

        def keep(h, first, rows):
            stat[slot, h, first:first + rows.shape[0], :] = rows
            sent[slot, h, first:first + rows.shape[0], :] = rows.astype(jnp.bfloat16)

        pack(top, bottom, keep)
        if slot == 0:
            pl.semaphore_wait(barrier, GREETED)
        for k in range(3):
            @pl.when(role[slot] == k + 1)
            def _():
                for index in range(len(PARTS)):
                    send_near(slot, k, index).start()
                    send_near(slot, k + 3, index).start()

        @pl.when(role[slot] == 0)
        def _():
            for index in range(len(PARTS)):
                send_near(slot, 6, index).start()

    grad_sq = total_square(own[0, 0].astype(jnp.float32)) + total_square(own[0, 1].astype(jnp.float32))

    @pl.when(leads)
    def _():
        for index in range(len(PARTS)):
            for k in range(7):
                send_near(0, k, index).wait_recv()
            total = stat[lead_slot, line, part(index)]
            for k in range(7):
                total += near[k, part(index)].astype(jnp.float32)
            both[line, part(index)] = total
            mine[part(index)] = total.astype(jnp.bfloat16)
            for k in range(3):
                @pl.when(lead_place == LEADERS[k] % RING)
                def _():
                    send_far(k, index).start()

    @pl.when(is_root)
    def _():
        for index in range(len(PARTS)):
            for k in range(3):
                send_far(k, index).wait_recv()
            total = both[line, part(index)]
            for k in range(3):
                total += far[k, part(index)].astype(jnp.float32)
            both[line, part(index)] = total
            mine[part(index)] = total.astype(jnp.bfloat16)
            send_across(index).start()
        for index in range(len(PARTS)):
            send_across(index).wait_recv()
            both[1 - line, part(index)] = across[part(index)].astype(jnp.float32)
        unpack(both, full)
        top, bottom = inverse_root(full[...])

        def keep(h, first, rows):
            fresh[lead_slot, h, first:first + rows.shape[0], :] = rows.astype(jnp.bfloat16)

        pack(top, bottom, keep)
        for index in range(len(PARTS)):
            for k in range(9):
                send_fresh(lead_slot, line, k, index).start()

    @pl.when(passes_on)
    def _():
        for index in range(len(PARTS)):
            send_fresh(lead_slot, line, 0, index).wait_recv()
            for k in range(3, 10):
                send_fresh(lead_slot, line, k, index).start()

    loads[3].wait()
    for slot in range(2):
        for half in range(2):
            @pl.when(jnp.logical_or(role[slot] != 0, jnp.logical_and(place[slot] != 0, line != half)))
            def _():
                for index in range(len(PARTS)):
                    send_fresh(slot, half, 0, index).wait_recv()
        unpack(fresh.at[slot], roots.at[slot])

    pre_sq = jnp.zeros((1, 1), jnp.float32)
    unscaled = []
    for b in range(2):
        left, right = (
            jnp.where(items[0] == k, roots[0], jnp.where(items[1] == k, roots[1], old[k])) for k in (2 * b, 2 * b + 1))
        done = jnp.dot(left, own[0, b], preferred_element_type=jnp.float32).astype(jnp.bfloat16)
        unscaled.append(jnp.dot(done, right, preferred_element_type=jnp.float32))
        pre_sq += total_square(unscaled[b])

    norms[mp] = jnp.where(positions(8, T)[0] == 0, grad_sq, pre_sq)

    def send_norm(k):
        return remote(norms.at[mp], norms.at[mp], norm_send.at[k], norm_recv.at[mp], (dp, lax.rem(mp + k, PEERS)))

    def recv_norm(k):
        source = lax.rem(mp + k, PEERS)
        return remote(norms.at[source], norms.at[source], norm_send.at[k], norm_recv.at[source], (dp, source))

    def start_norm(k, unused):
        send_norm(k).start()
        return unused

    def end_norm(k, unused):
        recv_norm(k).wait_recv()
        return unused

    def end_send(k, unused):
        send_norm(k).wait_send()
        return unused

    lax.fori_loop(1, PEERS, start_norm, 0)
    lax.fori_loop(1, PEERS, end_norm, 0)
    total = norms[0]
    for k in range(1, PEERS):
        total += norms[k]
    factor = jnp.sqrt(total[0:1, 0:1] / (total[1:2, 0:1] + 1e-06))
    for b in range(2):
        out[0, b] = (unscaled[b] * factor).astype(jnp.bfloat16)

    lax.fori_loop(1, PEERS, end_send, 0)
    for index in range(len(PARTS)):
        for slot in range(2):
            @pl.when(role[slot] != 0)
            def _():
                send_near(slot, 0, index).wait_send()
            send_near(slot, 3, index).wait_send()

        @pl.when(is_root)
        def _():
            send_across(index).wait_send()
            for k in range(9):
                send_fresh(lead_slot, line, k, index).wait_send()

        @pl.when(passes_on)
        def _():
            send_far(0, index).wait_send()
            for k in range(3, 10):
                send_fresh(lead_slot, line, k, index).wait_send()


def body(grads, order, offset, prev_roots):
    bf16, f32 = jnp.bfloat16, jnp.float32
    dma, parts = pltpu.SemaphoreType.DMA, len(PARTS)
    return pl.pallas_call(
        kernel,
        out_shape=jax.ShapeDtypeStruct((1, 2, N, N), bf16),
        in_specs=[pl.BlockSpec(memory_space=pl.ANY)] * 4,
        out_specs=pl.BlockSpec(memory_space=pltpu.VMEM),
        scratch_shapes=[
            pltpu.SMEM((1, 4), jnp.int32),
            pltpu.SMEM((1,), jnp.int32),
            pltpu.VMEM((1, 2, N, N), bf16),
            pltpu.VMEM((4, N, N), bf16),
            pltpu.VMEM((2, 2, HALF, T), f32),
            pltpu.VMEM((2, 2, HALF, T), bf16),
            pltpu.VMEM((7, HALF, T), bf16),
            pltpu.VMEM((HALF, T), bf16),
            pltpu.VMEM((3, HALF, T), bf16),
            pltpu.VMEM((HALF, T), bf16),
            pltpu.VMEM((2, HALF, T), f32),
            pltpu.VMEM((2, 2, HALF, T), bf16),
            pltpu.VMEM((N, N), f32),
            pltpu.VMEM((2, N, N), bf16),
            pltpu.VMEM((PEERS, 8, T), f32),
            dma, dma, dma, dma,
            dma((2, 2, parts)), dma((7, parts)),
            dma((parts,)), dma((3, parts)),
            dma((parts,)), dma((parts,)),
            dma((10, parts)), dma((2, 2, parts)),
            dma((PEERS,)), dma((PEERS,)),
        ],
        compiler_params=pltpu.CompilerParams(
            collective_id=0, has_side_effects=True, vmem_limit_bytes=60 * 1024 * 1024),
        cost_estimate=pl.CostEstimate(flops=10 * 2 * N ** 3, bytes_accessed=4 * 1024 * 1024, transcendentals=0),
        name="refresh",
    )(order, offset, grads, prev_roots)


def solution(mesh):
    placed = (P("dp", "mp", None, None), P("mp", None), P("mp"), P("mp", None, None))
    return jax.shard_map(
        body, mesh=mesh, in_specs=placed, out_specs=P("dp", "mp", None, None), check_vma=False
    )
```

```python
import jax
import jax.numpy as jnp
from jax import lax
from jax.experimental import pallas as pl
from jax.experimental.pallas import tpu as pltpu
from jax.sharding import PartitionSpec as P

MESH = pl.DeviceIdType.MESH
N = 512
T = 128
REPLICAS = 32
RING = 16
PEERS = 16
RIDGE = 0.1
ABOVE = (((0, 1), (0, 2), (0, 3)), ((1, 2), (1, 3), (2, 3)))
HALF = 4 * T + 16
PARTS = ((0, 256), (256, 272))
MEMBERS = (1, 2, -1)
LEADERS = (4, -4, 8)
NORM_PEERS = [(1, 2, 1), (1, 2, 0), (1, 1, 1), (1, 3, 1), (1, 1, 0), (1, 3, 0), (1, 0, 1), (1, 0, 0),
              (0, 2, 1), (0, 2, 0), (0, 1, 1), (0, 3, 1), (0, 1, 0), (0, 3, 0), (0, 0, 1)]


def part(index):
    return pl.ds(*PARTS[index])


def small(a, b):
    return jnp.dot(a.astype(jnp.bfloat16), b.astype(jnp.bfloat16), preferred_element_type=jnp.float32)


def total_square(value):
    return jnp.sum(jnp.sum(value * value, axis=0, keepdims=True), axis=1, keepdims=True)


def positions(rows, columns):
    shape = (rows, columns)
    return lax.broadcasted_iota(jnp.int32, shape, 0), lax.broadcasted_iota(jnp.int32, shape, 1)


def pack(top, bottom, store):
    row, column = positions(T, T)
    for h in range(2):
        tile = lambda i, j: (top[i * T:(i + 1) * T, j * T:(j + 1) * T] if i < 2 else
                             bottom[(i - 2) * T:(i - 1) * T, (j - 2) * T:(j - 1) * T])
        first, second = tile(2 * h, 2 * h), tile(2 * h + 1, 2 * h + 1)
        store(h, 0, jnp.where(column >= row, first, second))
        for index, (i, j) in enumerate(ABOVE[h]):
            store(h, (index + 1) * T, tile(i, j))
        diagonal = jnp.sum(jnp.where(column == row, second, 0.0), axis=0, keepdims=True)
        store(h, 4 * T, jnp.broadcast_to(diagonal, (16, T)))


def unpack(packed, full):
    row, column = positions(T, T)
    for h in range(2):
        both = packed[h, 0:T, :].astype(jnp.float32)
        mirrored = both.T
        diagonal = packed[h, 4 * T:4 * T + 16, :].astype(jnp.float32)[0:1]
        first = jnp.where(column >= row, both, mirrored)
        second = jnp.where(column < row, both, jnp.where(column == row, diagonal, mirrored))
        for block, i in ((first, 2 * h), (second, 2 * h + 1)):
            full[i * T:(i + 1) * T, i * T:(i + 1) * T] = block.astype(full.dtype)
        for index, (i, j) in enumerate(ABOVE[h]):
            block = packed[h, (index + 1) * T:(index + 2) * T, :]
            full[i * T:(i + 1) * T, j * T:(j + 1) * T] = block
            full[j * T:(j + 1) * T, i * T:(i + 1) * T] = block.T


def next_state(a):
    e2 = (small(a, a) - 10.0 * a) * 0.0625
    e4 = 3.125 * e2 + small(e2, e2)
    return 2.44140625 * a + small(e4, a)


def inverse_root(stat):
    row, column = positions(N, N)
    eye = jnp.where(row == column, 1.0, 0.0)
    ridged = stat * (1.0 / (N * REPLICAS)) + RIDGE * eye
    start = 2.5 / jnp.sqrt(total_square(ridged))
    a = start * ridged
    b = next_state(a)
    c = next_state(b)
    g = small(a, b) * 0.0625 - 0.3125 * (a + b)
    scale = jnp.sqrt(jnp.sqrt(start))
    top, bottom = (
        scale * (1.953125 * eye[rows, columns] + 1.25 * g[rows, columns] - 0.390625 * c[rows, columns]
                 - 0.25 * small(g[rows], c[:, columns]))
        for rows, columns in ((slice(0, 256), slice(0, N)), (slice(256, N), slice(256, N))))
    return top, bottom


def kernel(order, offset, grads, prev, out, order_here, offset_here, own, old, stat, sent, near, mine, mine_all, far, across, both, fresh,
           full, roots, norms, order_sem, offset_sem, own_sem, old_sem, near_send, near_recv, far_send, far_recv, across_send,
           across_recv, fresh_send, fresh_recv, norm_send, norm_recv, four_ready, eight_ready, peers_ready):
    dp, mp = lax.axis_index("dp"), lax.axis_index("mp")
    z, line, core = dp // 2, dp % 2, mp % 2
    sign = 1 - 2 * core

    loads = [pltpu.make_async_copy(*refs) for refs in (
        (order, order_here, order_sem), (offset, offset_here, offset_sem), (grads, own, own_sem), (prev, old, old_sem))]
    for load in loads:
        load.start()

    def along(step, flip=False):
        there = lax.rem(dp + 2 * step + 2 * RING, 2 * RING)
        return (there + 1 - 2 * line if flip else there, mp)

    def peer(y_step, x_step, core_step):
        return (dp, (1 - mp // 8 if y_step else mp // 8) * 8 + (mp // 2 + x_step) % 4 * 2 + (1 - core if core_step else core))

    def signal(semaphore, device):
        pl.semaphore_signal(semaphore, inc=1, device_id=device, device_id_type=MESH)

    barrier = pltpu.get_barrier_semaphore()
    greeted = [along(step) for step in (2, -2, 1, -1)] + [along(step, True) for step in (2, -2, 1, -1, 0)]
    greeted += [peer(1, 0, 0)] + [peer(*steps) for steps in NORM_PEERS if not steps[0]]
    for device in greeted:
        signal(barrier, device)

    role = [(sign * (z - 2 * slot - core) + 2 * RING) % 4 for slot in range(2)]
    leads = jnp.logical_or(role[0] == 0, role[1] == 0)
    lead_slot = jnp.where(role[1] == 0, 1, 0)

    def remote(source, target, send_sem, recv_sem, device):
        return pltpu.make_async_remote_copy(
            src_ref=source, dst_ref=target, send_sem=send_sem, recv_sem=recv_sem, device_id=device, device_id_type=MESH)

    def send_near(slot, k, index):
        half = line if k < 3 else 1 - line
        device = along(0 if k == 6 else -sign * MEMBERS[k % 3], k >= 3)
        return remote(sent.at[slot, half, part(index)], near.at[k, part(index)],
                      near_send.at[slot, 0 if k < 3 else 1, index], near_recv.at[k, index], device)

    def send_far(k, index):
        return remote(mine.at[part(index)], far.at[k, part(index)], far_send.at[k, index], far_recv.at[k, index],
                      along(LEADERS[k]))

    def send_across(index):
        return remote(mine_all.at[part(index)], across.at[part(index)], across_send.at[index], across_recv.at[index],
                      along(0, True))

    def send_fresh(slot, half, k, index):
        return remote(fresh.at[slot, half, part(index)], fresh.at[slot, half, part(index)], fresh_send.at[k, index],
                      fresh_recv.at[slot, half, index], along(sign * MEMBERS[k % 3], k >= 3))

    loads[0].wait()
    loads[1].wait()
    items = [order_here[0, (offset_here[0] + slot) % 4] for slot in range(2)]
    loads[2].wait()
    for slot in range(2):
        item = items[slot]
        picked = own[0, item // 2]
        turned = jnp.where(item % 2 == 0, picked, picked.T)
        top, bottom = (
            lax.dot_general(a, b, (((1,), (1,)), ((), ())), preferred_element_type=jnp.float32)
            for a, b in ((turned[:256], turned), (turned[256:], turned[256:])))

        def keep(h, first, rows):
            stat[slot, h, first:first + rows.shape[0], :] = rows
            sent[slot, h, first:first + rows.shape[0], :] = rows.astype(jnp.bfloat16)

        pack(top, bottom, keep)
        if slot == 0:
            pl.semaphore_wait(barrier, len(greeted))
        for k in range(3):
            @pl.when(role[slot] == k + 1)
            def _():
                for index in range(len(PARTS)):
                    send_near(slot, k, index).start()
                    send_near(slot, k + 3, index).start()

        @pl.when(role[slot] == 0)
        def _():
            for index in range(len(PARTS)):
                send_near(slot, 6, index).start()

    for step in (2, -2):
        signal(four_ready, along(step))
    signal(peers_ready, peer(1, 0, 0))
    grad_sq = total_square(own[0, 0].astype(jnp.float32)) + total_square(own[0, 1].astype(jnp.float32))
    pl.semaphore_wait(four_ready, 2)
    for step in (4, -4):
        signal(eight_ready, along(step))
    pl.semaphore_wait(eight_ready, 2)

    @pl.when(leads)
    def _():
        for index in range(len(PARTS)):
            for k in range(7):
                send_near(0, k, index).wait_recv()
            total = stat[lead_slot, line, part(index)]
            for k in range(7):
                total += near[k, part(index)].astype(jnp.float32)
            both[line, part(index)] = total
            mine[part(index)] = total.astype(jnp.bfloat16)
            for k in (2, 0, 1):
                send_far(k, index).start()
        for index in range(len(PARTS)):
            for k in range(3):
                send_far(k, index).wait_recv()
            total = both[line, part(index)]
            for k in range(3):
                total += far[k, part(index)].astype(jnp.float32)
            both[line, part(index)] = total
            mine_all[part(index)] = total.astype(jnp.bfloat16)
            send_across(index).start()
        for index in range(len(PARTS)):
            send_across(index).wait_recv()
            both[1 - line, part(index)] = across[part(index)].astype(jnp.float32)
        unpack(both, full)
        top, bottom = inverse_root(full[...])

        def keep(h, first, rows):
            fresh[lead_slot, h, first:first + rows.shape[0], :] = rows.astype(jnp.bfloat16)

        pack(top, bottom, keep)
        for index in range(len(PARTS)):
            for k in range(6):
                send_fresh(lead_slot, line, k, index).start()

    loads[3].wait()
    for slot in range(2):
        @pl.when(role[slot] != 0)
        def _():
            for index in range(len(PARTS)):
                for half in range(2):
                    send_fresh(slot, half, 0, index).wait_recv()
        unpack(fresh.at[slot], roots.at[slot])

    pre_sq = jnp.zeros((1, 1), jnp.float32)
    unscaled = []
    for b in range(2):
        left, right = (
            jnp.where(items[0] == k, roots[0], jnp.where(items[1] == k, roots[1], old[k])) for k in (2 * b, 2 * b + 1))
        done = jnp.dot(left, own[0, b], preferred_element_type=jnp.float32).astype(jnp.bfloat16)
        unscaled.append(jnp.dot(done, right, preferred_element_type=jnp.float32))
        pre_sq += total_square(unscaled[b])

    norms[mp] = jnp.where(positions(8, T)[0] == 0, grad_sq, pre_sq)

    def send_norm(k):
        return remote(norms.at[mp], norms.at[mp], norm_send.at[k], norm_recv.at[mp], peer(*NORM_PEERS[k]))

    def recv_norm(k):
        device = peer(*NORM_PEERS[k])
        return remote(norms.at[device[1]], norms.at[device[1]], norm_send.at[k], norm_recv.at[device[1]], device)

    pl.semaphore_wait(peers_ready, 1)
    for k in range(PEERS - 1):
        send_norm(k).start()
    for k in range(PEERS - 1):
        recv_norm(k).wait_recv()
    total = norms[0]
    for k in range(1, PEERS):
        total += norms[k]
    factor = jnp.sqrt(total[0:1, 0:1] / (total[1:2, 0:1] + 1e-06))
    for b in range(2):
        out[0, b] = (unscaled[b] * factor).astype(jnp.bfloat16)

    for k in range(PEERS - 1):
        send_norm(k).wait_send()
    for index in range(len(PARTS)):
        for slot in range(2):
            @pl.when(role[slot] != 0)
            def _():
                send_near(slot, 0, index).wait_send()
            send_near(slot, 3, index).wait_send()

        @pl.when(leads)
        def _():
            send_across(index).wait_send()
            for k in range(3):
                send_far(k, index).wait_send()
            for k in range(6):
                send_fresh(lead_slot, line, k, index).wait_send()


def body(grads, order, offset, prev_roots):
    bf16, f32 = jnp.bfloat16, jnp.float32
    dma, parts = pltpu.SemaphoreType.DMA, len(PARTS)
    return pl.pallas_call(
        kernel,
        out_shape=jax.ShapeDtypeStruct((1, 2, N, N), bf16),
        in_specs=[pl.BlockSpec(memory_space=pl.ANY)] * 4,
        out_specs=pl.BlockSpec(memory_space=pltpu.VMEM),
        scratch_shapes=[
            pltpu.SMEM((1, 4), jnp.int32),
            pltpu.SMEM((1,), jnp.int32),
            pltpu.VMEM((1, 2, N, N), bf16),
            pltpu.VMEM((4, N, N), bf16),
            pltpu.VMEM((2, 2, HALF, T), f32),
            pltpu.VMEM((2, 2, HALF, T), bf16),
            pltpu.VMEM((7, HALF, T), bf16),
            pltpu.VMEM((HALF, T), bf16),
            pltpu.VMEM((HALF, T), bf16),
            pltpu.VMEM((3, HALF, T), bf16),
            pltpu.VMEM((HALF, T), bf16),
            pltpu.VMEM((2, HALF, T), f32),
            pltpu.VMEM((2, 2, HALF, T), bf16),
            pltpu.VMEM((N, N), f32),
            pltpu.VMEM((2, N, N), bf16),
            pltpu.VMEM((PEERS, 8, T), f32),
            dma, dma, dma, dma,
            dma((2, 2, parts)), dma((7, parts)),
            dma((3, parts)), dma((3, parts)),
            dma((parts,)), dma((parts,)),
            dma((6, parts)), dma((2, 2, parts)),
            dma((PEERS,)), dma((PEERS,)),
            pltpu.SemaphoreType.REGULAR, pltpu.SemaphoreType.REGULAR, pltpu.SemaphoreType.REGULAR,
        ],
        compiler_params=pltpu.CompilerParams(
            collective_id=0, has_side_effects=True, vmem_limit_bytes=60 * 1024 * 1024),
        cost_estimate=pl.CostEstimate(flops=10 * 2 * N ** 3, bytes_accessed=4 * 1024 * 1024, transcendentals=0),
        name="refresh",
    )(order, offset, grads, prev_roots)


def solution(mesh):
    placed = (P("dp", "mp", None, None), P("mp", None), P("mp"), P("mp", None, None))
    return jax.shard_map(
        body, mesh=mesh, in_specs=placed, out_specs=P("dp", "mp", None, None), check_vma=False
    )
```

```python
import jax
import jax.numpy as jnp
from jax import lax
from jax.experimental import pallas as pl
from jax.experimental.pallas import tpu as pltpu
from jax.sharding import PartitionSpec as P

MESH = pl.DeviceIdType.MESH
N = 512
T = 128
REPLICAS = 32
RING = 16
PEERS = 16
RIDGE = 0.1
ABOVE = (((0, 1), (0, 2), (0, 3)), ((1, 2), (1, 3), (2, 3)))
HALF = 4 * T + 16
PARTS = ((0, 208), (208, 176), (384, 144))
MEMBERS = (1, 2, -1)
LEADERS = (4, -4, 8)
NORM_PEERS = [(1, 2, 1), (1, 2, 0), (1, 1, 1), (1, 3, 1), (1, 1, 0), (1, 3, 0), (1, 0, 1), (1, 0, 0),
              (0, 2, 1), (0, 2, 0), (0, 1, 1), (0, 3, 1), (0, 1, 0), (0, 3, 0), (0, 0, 1)]


def part(index):
    return pl.ds(*PARTS[index])


def small(a, b):
    return jnp.dot(a.astype(jnp.bfloat16), b.astype(jnp.bfloat16), preferred_element_type=jnp.float32)


def total_square(value):
    return jnp.sum(jnp.sum(value * value, axis=0, keepdims=True), axis=1, keepdims=True)


def positions(rows, columns):
    shape = (rows, columns)
    return lax.broadcasted_iota(jnp.int32, shape, 0), lax.broadcasted_iota(jnp.int32, shape, 1)


def pack(top, bottom, store):
    row, column = positions(T, T)
    for h in range(2):
        tile = lambda i, j: (top[i * T:(i + 1) * T, j * T:(j + 1) * T] if i < 2 else
                             bottom[(i - 2) * T:(i - 1) * T, (j - 2) * T:(j - 1) * T])
        first, second = tile(2 * h, 2 * h), tile(2 * h + 1, 2 * h + 1)
        store(h, 0, jnp.where(column >= row, first, second))
        for index, (i, j) in enumerate(ABOVE[h]):
            store(h, (index + 1) * T, tile(i, j))
        diagonal = jnp.sum(jnp.where(column == row, second, 0.0), axis=0, keepdims=True)
        store(h, 4 * T, jnp.broadcast_to(diagonal, (16, T)))


def unpack(packed, full):
    row, column = positions(T, T)
    for h in range(2):
        both = packed[h, 0:T, :].astype(jnp.float32)
        mirrored = both.T
        diagonal = packed[h, 4 * T:4 * T + 16, :].astype(jnp.float32)[0:1]
        first = jnp.where(column >= row, both, mirrored)
        second = jnp.where(column < row, both, jnp.where(column == row, diagonal, mirrored))
        for block, i in ((first, 2 * h), (second, 2 * h + 1)):
            full[i * T:(i + 1) * T, i * T:(i + 1) * T] = block.astype(full.dtype)
        for index, (i, j) in enumerate(ABOVE[h]):
            block = packed[h, (index + 1) * T:(index + 2) * T, :]
            full[i * T:(i + 1) * T, j * T:(j + 1) * T] = block
            full[j * T:(j + 1) * T, i * T:(i + 1) * T] = block.T


def next_state(a):
    e2 = (small(a, a) - 10.0 * a) * 0.0625
    e4 = 3.125 * e2 + small(e2, e2)
    return 2.44140625 * a + small(e4, a)


def inverse_root(stat):
    row, column = positions(N, N)
    eye = jnp.where(row == column, 1.0, 0.0)
    ridged = stat * (1.0 / (N * REPLICAS)) + RIDGE * eye
    start = 2.5 / jnp.sqrt(total_square(ridged))
    a = start * ridged
    b = next_state(a)
    c = next_state(b)
    g = small(a, b) * 0.0625 - 0.3125 * (a + b)
    scale = jnp.sqrt(jnp.sqrt(start))
    top, bottom = (
        scale * (1.953125 * eye[rows, columns] + 1.25 * g[rows, columns] - 0.390625 * c[rows, columns]
                 - 0.25 * small(g[rows], c[:, columns]))
        for rows, columns in ((slice(0, 256), slice(0, N)), (slice(256, N), slice(256, N))))
    return top, bottom


def kernel(order, offset, grads, prev, out, order_here, offset_here, own, old, stat, sent, near, mine, mine_all, far, across, both, fresh,
           full, roots, norms, order_sem, offset_sem, own_sem, old_sem, near_send, near_recv, far_send, far_recv, across_send,
           across_recv, fresh_send, fresh_recv, norm_send, norm_recv, four_ready, eight_ready, peers_ready):
    dp, mp = lax.axis_index("dp"), lax.axis_index("mp")
    z, line, core = dp // 2, dp % 2, mp % 2
    sign = 1 - 2 * core

    loads = [pltpu.make_async_copy(*refs) for refs in (
        (order, order_here, order_sem), (offset, offset_here, offset_sem), (grads, own, own_sem), (prev, old, old_sem))]
    for load in loads:
        load.start()

    def along(step, flip=False):
        there = lax.rem(dp + 2 * step + 2 * RING, 2 * RING)
        return (there + 1 - 2 * line if flip else there, mp)

    def peer(y_step, x_step, core_step):
        return (dp, (1 - mp // 8 if y_step else mp // 8) * 8 + (mp // 2 + x_step) % 4 * 2 + (1 - core if core_step else core))

    def signal(semaphore, device):
        pl.semaphore_signal(semaphore, inc=1, device_id=device, device_id_type=MESH)

    barrier = pltpu.get_barrier_semaphore()
    greeted = [along(step) for step in (2, -2, 1, -1)] + [along(step, True) for step in (2, -2, 1, -1, 0)]
    greeted += [peer(1, 0, 0)] + [peer(*steps) for steps in NORM_PEERS if not steps[0]]
    for device in greeted:
        signal(barrier, device)

    role = [(sign * (z - 2 * slot - core) + 2 * RING) % 4 for slot in range(2)]
    leads = jnp.logical_or(role[0] == 0, role[1] == 0)
    lead_slot = jnp.where(role[1] == 0, 1, 0)

    def remote(source, target, send_sem, recv_sem, device):
        return pltpu.make_async_remote_copy(
            src_ref=source, dst_ref=target, send_sem=send_sem, recv_sem=recv_sem, device_id=device, device_id_type=MESH)

    def send_near(slot, k, index):
        half = line if k < 3 else 1 - line
        device = along(0 if k == 6 else -sign * MEMBERS[k % 3], k >= 3)
        return remote(sent.at[slot, half, part(index)], near.at[k, part(index)],
                      near_send.at[slot, 0 if k < 3 else 1, index], near_recv.at[k, index], device)

    def send_far(k, index):
        return remote(mine.at[part(index)], far.at[k, part(index)], far_send.at[k, index], far_recv.at[k, index],
                      along(LEADERS[k]))

    def send_across(index):
        return remote(mine_all.at[part(index)], across.at[part(index)], across_send.at[index], across_recv.at[index],
                      along(0, True))

    def send_fresh(slot, half, k, index):
        return remote(fresh.at[slot, half, part(index)], fresh.at[slot, half, part(index)], fresh_send.at[half, k, index],
                      fresh_recv.at[slot, half, index], along(sign * MEMBERS[k]))

    loads[0].wait()
    loads[1].wait()
    items = [order_here[0, (offset_here[0] + slot) % 4] for slot in range(2)]
    loads[2].wait()
    for slot in range(2):
        item = items[slot]
        picked = own[0, item // 2]
        turned = jnp.where(item % 2 == 0, picked, picked.T)
        top, bottom = (
            lax.dot_general(a, b, (((1,), (1,)), ((), ())), preferred_element_type=jnp.float32)
            for a, b in ((turned[:256], turned), (turned[256:], turned[256:])))

        def keep(h, first, rows):
            stat[slot, h, first:first + rows.shape[0], :] = rows
            sent[slot, h, first:first + rows.shape[0], :] = rows.astype(jnp.bfloat16)

        pack(top, bottom, keep)
        if slot == 0:
            pl.semaphore_wait(barrier, len(greeted))
        for k in range(3):
            @pl.when(role[slot] == k + 1)
            def _():
                for index in range(len(PARTS)):
                    send_near(slot, k, index).start()
                    send_near(slot, k + 3, index).start()

        @pl.when(role[slot] == 0)
        def _():
            for index in range(len(PARTS)):
                send_near(slot, 6, index).start()

    for step in (2, -2):
        signal(four_ready, along(step))
    signal(peers_ready, peer(1, 0, 0))
    grad_sq = total_square(own[0, 0].astype(jnp.float32)) + total_square(own[0, 1].astype(jnp.float32))
    pl.semaphore_wait(four_ready, 2)
    for step in (4, -4):
        signal(eight_ready, along(step))
    pl.semaphore_wait(eight_ready, 2)

    @pl.when(leads)
    def _():
        for index in range(len(PARTS)):
            for k in range(7):
                send_near(0, k, index).wait_recv()
            total = stat[lead_slot, line, part(index)]
            for k in range(7):
                total += near[k, part(index)].astype(jnp.float32)
            both[line, part(index)] = total
            mine[part(index)] = total.astype(jnp.bfloat16)
            for k in (2, 0, 1):
                send_far(k, index).start()
        for index in range(len(PARTS)):
            for k in range(3):
                send_far(k, index).wait_recv()
            total = both[line, part(index)]
            for k in range(3):
                total += far[k, part(index)].astype(jnp.float32)
            both[line, part(index)] = total
            mine_all[part(index)] = total.astype(jnp.bfloat16)
            send_across(index).start()
        for index in range(len(PARTS)):
            send_across(index).wait_recv()
            both[1 - line, part(index)] = across[part(index)].astype(jnp.float32)
        unpack(both, full)
        top, bottom = inverse_root(full[...])

        def keep(h, first, rows):
            fresh[lead_slot, h, first:first + rows.shape[0], :] = rows.astype(jnp.bfloat16)

        pack(top, bottom, keep)
        for half in range(2):
            for index in range(len(PARTS)):
                for k in range(3):
                    send_fresh(lead_slot, half, k, index).start()

    loads[3].wait()
    for slot in range(2):
        @pl.when(role[slot] != 0)
        def _():
            for index in range(len(PARTS)):
                for half in range(2):
                    send_fresh(slot, half, 0, index).wait_recv()
        unpack(fresh.at[slot], roots.at[slot])

    pre_sq = jnp.zeros((1, 1), jnp.float32)
    unscaled = []
    for b in range(2):
        left, right = (
            jnp.where(items[0] == k, roots[0], jnp.where(items[1] == k, roots[1], old[k])) for k in (2 * b, 2 * b + 1))
        done = jnp.dot(left, own[0, b], preferred_element_type=jnp.float32).astype(jnp.bfloat16)
        unscaled.append(jnp.dot(done, right, preferred_element_type=jnp.float32))
        pre_sq += total_square(unscaled[b])

    norms[mp] = jnp.where(positions(8, T)[0] == 0, grad_sq, pre_sq)

    def send_norm(k):
        return remote(norms.at[mp], norms.at[mp], norm_send.at[k], norm_recv.at[mp], peer(*NORM_PEERS[k]))

    def recv_norm(k):
        device = peer(*NORM_PEERS[k])
        return remote(norms.at[device[1]], norms.at[device[1]], norm_send.at[k], norm_recv.at[device[1]], device)

    pl.semaphore_wait(peers_ready, 1)
    for k in range(PEERS - 1):
        send_norm(k).start()
    for k in range(PEERS - 1):
        recv_norm(k).wait_recv()
    total = norms[0]
    for k in range(1, PEERS):
        total += norms[k]
    factor = jnp.sqrt(total[0:1, 0:1] / (total[1:2, 0:1] + 1e-06))
    for b in range(2):
        out[0, b] = (unscaled[b] * factor).astype(jnp.bfloat16)

    for k in range(PEERS - 1):
        send_norm(k).wait_send()
    for index in range(len(PARTS)):
        for slot in range(2):
            @pl.when(role[slot] != 0)
            def _():
                send_near(slot, 0, index).wait_send()
            send_near(slot, 3, index).wait_send()

        @pl.when(leads)
        def _():
            send_across(index).wait_send()
            for k in range(3):
                send_far(k, index).wait_send()
            for half in range(2):
                for k in range(3):
                    send_fresh(lead_slot, half, k, index).wait_send()


def pinned(array):
    return pltpu.with_memory_space_constraint(array, pltpu.HBM)


def body(grads, order, offset, prev_roots):
    bf16, f32 = jnp.bfloat16, jnp.float32
    dma, parts = pltpu.SemaphoreType.DMA, len(PARTS)
    return pl.pallas_call(
        kernel,
        out_shape=jax.ShapeDtypeStruct((1, 2, N, N), bf16),
        in_specs=[pl.BlockSpec(memory_space=pl.ANY)] * 4,
        out_specs=pl.BlockSpec(memory_space=pltpu.VMEM),
        scratch_shapes=[
            pltpu.SMEM((1, 4), jnp.int32),
            pltpu.SMEM((1,), jnp.int32),
            pltpu.VMEM((1, 2, N, N), bf16),
            pltpu.VMEM((4, N, N), bf16),
            pltpu.VMEM((2, 2, HALF, T), f32),
            pltpu.VMEM((2, 2, HALF, T), bf16),
            pltpu.VMEM((7, HALF, T), bf16),
            pltpu.VMEM((HALF, T), bf16),
            pltpu.VMEM((HALF, T), bf16),
            pltpu.VMEM((3, HALF, T), bf16),
            pltpu.VMEM((HALF, T), bf16),
            pltpu.VMEM((2, HALF, T), f32),
            pltpu.VMEM((2, 2, HALF, T), bf16),
            pltpu.VMEM((N, N), f32),
            pltpu.VMEM((2, N, N), bf16),
            pltpu.VMEM((PEERS, 8, T), f32),
            dma, dma, dma, dma,
            dma((2, 2, parts)), dma((7, parts)),
            dma((3, parts)), dma((3, parts)),
            dma((parts,)), dma((parts,)),
            dma((2, 3, parts)), dma((2, 2, parts)),
            dma((PEERS,)), dma((PEERS,)),
            pltpu.SemaphoreType.REGULAR, pltpu.SemaphoreType.REGULAR, pltpu.SemaphoreType.REGULAR,
        ],
        compiler_params=pltpu.CompilerParams(
            collective_id=0, has_side_effects=True, vmem_limit_bytes=40 * 1024 * 1024),
        cost_estimate=pl.CostEstimate(flops=10 * 2 * N ** 3, bytes_accessed=4 * 1024 * 1024, transcendentals=0),
        name="refresh",
    )(pinned(order), offset, pinned(grads), pinned(prev_roots))


def solution(mesh):
    placed = (P("dp", "mp", None, None), P("mp", None), P("mp"), P("mp", None, None))
    return jax.shard_map(
        body, mesh=mesh, in_specs=placed, out_specs=P("dp", "mp", None, None), check_vma=False
    )
```

```python
import jax
import jax.numpy as jnp
from jax import lax
from jax.experimental import pallas as pl
from jax.experimental.pallas import tpu as pltpu
from jax.sharding import PartitionSpec as P

MESH = pl.DeviceIdType.MESH
N = 512
T = 128
REPLICAS = 32
RING = 16
PEERS = 16
RIDGE = 0.1
ABOVE = (((0, 1), (0, 2), (0, 3)), ((1, 2), (1, 3), (2, 3)))
HALF = 4 * T + 16
PARTS = ((0, 208), (208, 176), (384, 144))
MEMBERS = (1, 2, -1)
NORM_PEERS = [(1, 2, 1), (1, 2, 0), (1, 1, 1), (1, 3, 1), (1, 1, 0), (1, 3, 0), (1, 0, 1), (1, 0, 0),
              (0, 2, 1), (0, 2, 0), (0, 1, 1), (0, 3, 1), (0, 1, 0), (0, 3, 0), (0, 0, 1)]


def part(index):
    return pl.ds(*PARTS[index])


def small(a, b):
    return jnp.dot(a.astype(jnp.bfloat16), b.astype(jnp.bfloat16), preferred_element_type=jnp.float32)


def total_square(value):
    return jnp.sum(jnp.sum(value * value, axis=0, keepdims=True), axis=1, keepdims=True)


def positions(rows, columns):
    shape = (rows, columns)
    return lax.broadcasted_iota(jnp.int32, shape, 0), lax.broadcasted_iota(jnp.int32, shape, 1)


def pack(top, bottom, store):
    row, column = positions(T, T)
    for h in range(2):
        tile = lambda i, j: (top[i * T:(i + 1) * T, j * T:(j + 1) * T] if i < 2 else
                             bottom[(i - 2) * T:(i - 1) * T, (j - 2) * T:(j - 1) * T])
        first, second = tile(2 * h, 2 * h), tile(2 * h + 1, 2 * h + 1)
        store(h, 0, jnp.where(column >= row, first, second))
        for index, (i, j) in enumerate(ABOVE[h]):
            store(h, (index + 1) * T, tile(i, j))
        diagonal = jnp.sum(jnp.where(column == row, second, 0.0), axis=0, keepdims=True)
        store(h, 4 * T, jnp.broadcast_to(diagonal, (16, T)))


def unpack(packed, full):
    row, column = positions(T, T)
    for h in range(2):
        both = packed[h, 0:T, :].astype(jnp.float32)
        mirrored = both.T
        diagonal = packed[h, 4 * T:4 * T + 16, :].astype(jnp.float32)[0:1]
        first = jnp.where(column >= row, both, mirrored)
        second = jnp.where(column < row, both, jnp.where(column == row, diagonal, mirrored))
        for block, i in ((first, 2 * h), (second, 2 * h + 1)):
            full[i * T:(i + 1) * T, i * T:(i + 1) * T] = block.astype(full.dtype)
        for index, (i, j) in enumerate(ABOVE[h]):
            block = packed[h, (index + 1) * T:(index + 2) * T, :]
            full[i * T:(i + 1) * T, j * T:(j + 1) * T] = block
            full[j * T:(j + 1) * T, i * T:(i + 1) * T] = block.T


def next_state(a):
    e2 = (small(a, a) - 10.0 * a) * 0.0625
    e4 = 3.125 * e2 + small(e2, e2)
    return 2.44140625 * a + small(e4, a)


def inverse_root(stat):
    row, column = positions(N, N)
    eye = jnp.where(row == column, 1.0, 0.0)
    ridged = stat * (1.0 / (N * REPLICAS)) + RIDGE * eye
    start = 2.5 / jnp.sqrt(total_square(ridged))
    a = start * ridged
    b = next_state(a)
    c = next_state(b)
    g = small(a, b) * 0.0625 - 0.3125 * (a + b)
    scale = jnp.sqrt(jnp.sqrt(start))
    top, bottom = (
        scale * (1.953125 * eye[rows, columns] + 1.25 * g[rows, columns] - 0.390625 * c[rows, columns]
                 - 0.25 * small(g[rows], c[:, columns]))
        for rows, columns in ((slice(0, 256), slice(0, N)), (slice(256, N), slice(256, N))))
    return top, bottom


def kernel(order, offset, grads, prev, out, order_here, offset_here, own, old, stat, sent, near, mine, far, across, both, fresh,
           full, roots, norms, order_sem, offset_sem, own_sem, old_sem, near_send, near_recv, far_send, far_recv, across_send,
           across_recv, fresh_send, fresh_recv, norm_send, norm_recv, four_ready, peers_ready):
    dp, mp = lax.axis_index("dp"), lax.axis_index("mp")
    z, line, core = dp // 2, dp % 2, mp % 2
    sign = 1 - 2 * core

    loads = [pltpu.make_async_copy(*refs) for refs in (
        (order, order_here, order_sem), (offset, offset_here, offset_sem), (grads, own, own_sem), (prev, old, old_sem))]
    for load in loads:
        load.start()

    def along(step, flip=False):
        there = lax.rem(dp + 2 * step + 2 * RING, 2 * RING)
        return (there + 1 - 2 * line if flip else there, mp)

    def peer(y_step, x_step, core_step):
        return (dp, (1 - mp // 8 if y_step else mp // 8) * 8 + (mp // 2 + x_step) % 4 * 2 + (1 - core if core_step else core))

    def signal(semaphore, device):
        pl.semaphore_signal(semaphore, inc=1, device_id=device, device_id_type=MESH)

    barrier = pltpu.get_barrier_semaphore()
    greeted = [along(step) for step in (2, -2, 1, -1)] + [along(step, True) for step in (2, -2, 1, -1, 0)]
    greeted += [peer(1, 0, 0)] + [peer(*steps) for steps in NORM_PEERS if not steps[0]]
    for device in greeted:
        signal(barrier, device)

    role = [(sign * (z - 2 * slot - core) + 2 * RING) % 4 for slot in range(2)]
    leads = jnp.logical_or(role[0] == 0, role[1] == 0)
    lead_slot = jnp.where(role[1] == 0, 1, 0)

    def remote(source, target, send_sem, recv_sem, device):
        return pltpu.make_async_remote_copy(
            src_ref=source, dst_ref=target, send_sem=send_sem, recv_sem=recv_sem, device_id=device, device_id_type=MESH)

    def send_near(slot, k, index):
        half = line if k < 3 else 1 - line
        device = along(0 if k == 6 else -sign * MEMBERS[k % 3], k >= 3)
        return remote(sent.at[slot, half, part(index)], near.at[k, part(index)],
                      near_send.at[slot, 0 if k < 3 else 1, index], near_recv.at[k, index], device)

    first_side = 4 - 8 * ((z // 4 + core) % 2)

    def send_far(k, index):
        return remote(mine.at[k, part(index)], far.at[k, part(index)], far_send.at[k, index], far_recv.at[k, index],
                      along(first_side if k == 0 else -first_side))

    def send_across(index):
        return remote(mine.at[2, part(index)], across.at[part(index)], across_send.at[index], across_recv.at[index],
                      along(0, True))

    def send_fresh(slot, half, k, index):
        return remote(fresh.at[slot, half, part(index)], fresh.at[slot, half, part(index)], fresh_send.at[half, k, index],
                      fresh_recv.at[slot, half, index], along(sign * MEMBERS[k]))

    loads[0].wait()
    loads[1].wait()
    items = [order_here[0, (offset_here[0] + slot) % 4] for slot in range(2)]
    loads[2].wait()
    for slot in range(2):
        item = items[slot]
        picked = own[0, item // 2]
        turned = jnp.where(item % 2 == 0, picked, picked.T)
        top, bottom = (
            lax.dot_general(a, b, (((1,), (1,)), ((), ())), preferred_element_type=jnp.float32)
            for a, b in ((turned[:256], turned), (turned[256:], turned[256:])))

        def keep(h, first, rows):
            stat[slot, h, first:first + rows.shape[0], :] = rows
            sent[slot, h, first:first + rows.shape[0], :] = rows.astype(jnp.bfloat16)

        pack(top, bottom, keep)
        if slot == 0:
            pl.semaphore_wait(barrier, len(greeted))
        for k in range(3):
            @pl.when(role[slot] == k + 1)
            def _():
                for index in range(len(PARTS)):
                    send_near(slot, k, index).start()
                    send_near(slot, k + 3, index).start()

        @pl.when(role[slot] == 0)
        def _():
            for index in range(len(PARTS)):
                send_near(slot, 6, index).start()

    for step in (2, -2):
        signal(four_ready, along(step))
    signal(peers_ready, peer(1, 0, 0))
    grad_sq = total_square(own[0, 0].astype(jnp.float32)) + total_square(own[0, 1].astype(jnp.float32))
    pl.semaphore_wait(four_ready, 2)

    @pl.when(leads)
    def _():
        for index in range(len(PARTS)):
            for k in range(7):
                send_near(0, k, index).wait_recv()
            total = stat[lead_slot, line, part(index)]
            for k in range(7):
                total += near[k, part(index)].astype(jnp.float32)
            both[line, part(index)] = total
            mine[0, part(index)] = total.astype(jnp.bfloat16)
            send_far(0, index).start()
        for k in range(2):
            for index in range(len(PARTS)):
                send_far(k, index).wait_recv()
                total = both[line, part(index)] + far[k, part(index)].astype(jnp.float32)
                both[line, part(index)] = total
                mine[k + 1, part(index)] = total.astype(jnp.bfloat16)
                (send_far(1, index) if k == 0 else send_across(index)).start()
        for index in range(len(PARTS)):
            send_across(index).wait_recv()
            both[1 - line, part(index)] = across[part(index)].astype(jnp.float32)
        unpack(both, full)
        top, bottom = inverse_root(full[...])

        def keep(h, first, rows):
            fresh[lead_slot, h, first:first + rows.shape[0], :] = rows.astype(jnp.bfloat16)

        pack(top, bottom, keep)
        for half in range(2):
            for index in range(len(PARTS)):
                for k in range(3):
                    send_fresh(lead_slot, half, k, index).start()

    loads[3].wait()
    for slot in range(2):
        @pl.when(role[slot] != 0)
        def _():
            for index in range(len(PARTS)):
                for half in range(2):
                    send_fresh(slot, half, 0, index).wait_recv()
        unpack(fresh.at[slot], roots.at[slot])

    pre_sq = jnp.zeros((1, 1), jnp.float32)
    unscaled = []
    for b in range(2):
        left, right = (
            jnp.where(items[0] == k, roots[0], jnp.where(items[1] == k, roots[1], old[k])) for k in (2 * b, 2 * b + 1))
        done = jnp.dot(left, own[0, b], preferred_element_type=jnp.float32).astype(jnp.bfloat16)
        unscaled.append(jnp.dot(done, right, preferred_element_type=jnp.float32))
        pre_sq += total_square(unscaled[b])

    norms[mp] = jnp.where(positions(8, T)[0] == 0, grad_sq, pre_sq)

    def send_norm(k):
        return remote(norms.at[mp], norms.at[mp], norm_send.at[k], norm_recv.at[mp], peer(*NORM_PEERS[k]))

    def recv_norm(k):
        device = peer(*NORM_PEERS[k])
        return remote(norms.at[device[1]], norms.at[device[1]], norm_send.at[k], norm_recv.at[device[1]], device)

    pl.semaphore_wait(peers_ready, 1)
    for k in range(PEERS - 1):
        send_norm(k).start()
    for k in range(PEERS - 1):
        recv_norm(k).wait_recv()
    total = norms[0]
    for k in range(1, PEERS):
        total += norms[k]
    factor = jnp.sqrt(total[0:1, 0:1] / (total[1:2, 0:1] + 1e-06))
    for b in range(2):
        out[0, b] = (unscaled[b] * factor).astype(jnp.bfloat16)

    for k in range(PEERS - 1):
        send_norm(k).wait_send()
    for index in range(len(PARTS)):
        for slot in range(2):
            @pl.when(role[slot] != 0)
            def _():
                send_near(slot, 0, index).wait_send()
            send_near(slot, 3, index).wait_send()

        @pl.when(leads)
        def _():
            send_across(index).wait_send()
            for k in range(2):
                send_far(k, index).wait_send()
            for half in range(2):
                for k in range(3):
                    send_fresh(lead_slot, half, k, index).wait_send()


def pinned(array):
    return pltpu.with_memory_space_constraint(array, pltpu.HBM)


def body(grads, order, offset, prev_roots):
    bf16, f32 = jnp.bfloat16, jnp.float32
    dma, parts = pltpu.SemaphoreType.DMA, len(PARTS)
    return pl.pallas_call(
        kernel,
        out_shape=jax.ShapeDtypeStruct((1, 2, N, N), bf16),
        in_specs=[pl.BlockSpec(memory_space=pl.ANY)] * 4,
        out_specs=pl.BlockSpec(memory_space=pltpu.VMEM),
        scratch_shapes=[
            pltpu.SMEM((1, 4), jnp.int32),
            pltpu.SMEM((1,), jnp.int32),
            pltpu.VMEM((1, 2, N, N), bf16),
            pltpu.VMEM((4, N, N), bf16),
            pltpu.VMEM((2, 2, HALF, T), f32),
            pltpu.VMEM((2, 2, HALF, T), bf16),
            pltpu.VMEM((7, HALF, T), bf16),
            pltpu.VMEM((3, HALF, T), bf16),
            pltpu.VMEM((2, HALF, T), bf16),
            pltpu.VMEM((HALF, T), bf16),
            pltpu.VMEM((2, HALF, T), f32),
            pltpu.VMEM((2, 2, HALF, T), bf16),
            pltpu.VMEM((N, N), f32),
            pltpu.VMEM((2, N, N), bf16),
            pltpu.VMEM((PEERS, 8, T), f32),
            dma, dma, dma, dma,
            dma((2, 2, parts)), dma((7, parts)),
            dma((2, parts)), dma((2, parts)),
            dma((parts,)), dma((parts,)),
            dma((2, 3, parts)), dma((2, 2, parts)),
            dma((PEERS,)), dma((PEERS,)),
            pltpu.SemaphoreType.REGULAR, pltpu.SemaphoreType.REGULAR,
        ],
        compiler_params=pltpu.CompilerParams(
            collective_id=0, has_side_effects=True, vmem_limit_bytes=40 * 1024 * 1024),
        cost_estimate=pl.CostEstimate(flops=10 * 2 * N ** 3, bytes_accessed=4 * 1024 * 1024, transcendentals=0),
        name="refresh",
    )(pinned(order), offset, pinned(grads), pinned(prev_roots))


def solution(mesh):
    placed = (P("dp", "mp", None, None), P("mp", None), P("mp"), P("mp", None, None))
    return jax.shard_map(
        body, mesh=mesh, in_specs=placed, out_specs=P("dp", "mp", None, None), check_vma=False
    )
```

```python
import jax
import jax.numpy as jnp
from jax import lax
from jax.experimental import pallas as pl
from jax.experimental.pallas import tpu as pltpu
from jax.sharding import PartitionSpec as P

MESH = pl.DeviceIdType.MESH
N = 512
T = 128
REPLICAS = 32
RING = 16
PEERS = 16
RIDGE = 0.1
ABOVE = (((0, 1), (0, 2), (0, 3)), ((1, 2), (1, 3), (2, 3)))
HALF = 4 * T + 16
PARTS = ((0, 208), (208, 176), (384, 144))
MEMBERS = (1, 2, -1)
NORM_PEERS = [(1, 2, 1), (1, 2, 0), (1, 1, 1), (1, 3, 1), (1, 1, 0), (1, 3, 0), (1, 0, 1), (1, 0, 0),
              (0, 2, 1), (0, 2, 0), (0, 1, 1), (0, 3, 1), (0, 1, 0), (0, 3, 0), (0, 0, 1)]


def part(index):
    return pl.ds(*PARTS[index])


def small(a, b):
    return jnp.dot(a.astype(jnp.bfloat16), b.astype(jnp.bfloat16), preferred_element_type=jnp.float32)


def total_square(value):
    return jnp.sum(jnp.sum(value * value, axis=0, keepdims=True), axis=1, keepdims=True)


def positions(rows, columns):
    shape = (rows, columns)
    return lax.broadcasted_iota(jnp.int32, shape, 0), lax.broadcasted_iota(jnp.int32, shape, 1)


def pack(top, bottom, store, halves=(0, 1)):
    row, column = positions(T, T)
    for h in halves:
        tile = lambda i, j: (top[i * T:(i + 1) * T, j * T:(j + 1) * T] if i < 2 else
                             bottom[(i - 2) * T:(i - 1) * T, (j - 2) * T:(j - 1) * T])
        first, second = tile(2 * h, 2 * h), tile(2 * h + 1, 2 * h + 1)
        store(h, 0, jnp.where(column >= row, first, second))
        for index, (i, j) in enumerate(ABOVE[h]):
            store(h, (index + 1) * T, tile(i, j))
        diagonal = jnp.sum(jnp.where(column == row, second, 0.0), axis=0, keepdims=True)
        store(h, 4 * T, jnp.broadcast_to(diagonal, (16, T)))


def unpack(packed, full):
    row, column = positions(T, T)
    for h in range(2):
        both = packed[h, 0:T, :].astype(jnp.float32)
        mirrored = both.T
        diagonal = packed[h, 4 * T:4 * T + 16, :].astype(jnp.float32)[0:1]
        first = jnp.where(column >= row, both, mirrored)
        second = jnp.where(column < row, both, jnp.where(column == row, diagonal, mirrored))
        for block, i in ((first, 2 * h), (second, 2 * h + 1)):
            full[i * T:(i + 1) * T, i * T:(i + 1) * T] = block.astype(full.dtype)
        for index, (i, j) in enumerate(ABOVE[h]):
            block = packed[h, (index + 1) * T:(index + 2) * T, :]
            full[i * T:(i + 1) * T, j * T:(j + 1) * T] = block
            full[j * T:(j + 1) * T, i * T:(i + 1) * T] = block.T


def next_state(a, square=None):
    e2 = ((small(a, a) if square is None else square) - 10.0 * a) * 0.0625
    e4 = 3.125 * e2 + small(e2, e2)
    return 2.44140625 * a + small(e4, a)


def inverse_root(stat):
    row, column = positions(N, N)
    eye = jnp.where(row == column, 1.0, 0.0)
    ridged = stat * (1.0 / (N * REPLICAS)) + RIDGE * eye
    square = small(ridged, ridged)
    start = 2.5 / jnp.sqrt(total_square(ridged))
    a = start * ridged
    b = next_state(a, (start * start) * square)
    c = next_state(b)
    g = small(a, b) * 0.0625 - 0.3125 * (a + b)
    scale = jnp.sqrt(jnp.sqrt(start))
    for rows, columns in ((slice(0, 256), slice(0, N)), (slice(256, N), slice(256, N))):
        yield scale * (1.953125 * eye[rows, columns] + 1.25 * g[rows, columns] - 0.390625 * c[rows, columns]
                       - 0.25 * small(g[rows], c[:, columns]))


def kernel(order, offset, grads, prev, out, order_here, offset_here, own, stat, sent, near, mine, far, across, both, fresh,
           full, roots, norms, order_sem, offset_sem, own_sem, old_sem, near_send, near_recv, far_send, far_recv, across_send,
           across_recv, fresh_send, fresh_recv, norm_send, norm_recv, four_ready, peers_ready):
    dp, mp = lax.axis_index("dp"), lax.axis_index("mp")
    z, line, core = dp // 2, dp % 2, mp % 2
    sign = 1 - 2 * core

    loads = [pltpu.make_async_copy(*refs) for refs in (
        (order, order_here, order_sem), (offset, offset_here, offset_sem), (grads, own, own_sem), (prev, roots.at[pl.ds(0, 4)], old_sem))]
    for load in loads:
        load.start()

    def along(step, flip=False):
        there = lax.rem(dp + 2 * step + 2 * RING, 2 * RING)
        return (there + 1 - 2 * line if flip else there, mp)

    def peer(y_step, x_step, core_step):
        return (dp, (1 - mp // 8 if y_step else mp // 8) * 8 + (mp // 2 + x_step) % 4 * 2 + (1 - core if core_step else core))

    def signal(semaphore, device):
        pl.semaphore_signal(semaphore, inc=1, device_id=device, device_id_type=MESH)

    barrier = pltpu.get_barrier_semaphore()
    greeted = [along(step) for step in (2, -2, 1, -1)] + [along(step, True) for step in (2, -2, 1, -1, 0)]
    greeted += [peer(1, 0, 0)] + [peer(*steps) for steps in NORM_PEERS if not steps[0]]
    for device in greeted:
        signal(barrier, device)

    role = [(sign * (z - 2 * slot - core) + 2 * RING) % 4 for slot in range(2)]
    leads = jnp.logical_or(role[0] == 0, role[1] == 0)
    lead_slot = jnp.where(role[1] == 0, 1, 0)

    def remote(source, target, send_sem, recv_sem, device):
        return pltpu.make_async_remote_copy(
            src_ref=source, dst_ref=target, send_sem=send_sem, recv_sem=recv_sem, device_id=device, device_id_type=MESH)

    def send_near(slot, k, index):
        half = line if k < 3 else 1 - line
        device = along(0 if k == 6 else -sign * MEMBERS[k % 3], k >= 3)
        return remote(sent.at[slot, half, part(index)], near.at[k, part(index)],
                      near_send.at[slot, 0 if k < 3 else 1, index], near_recv.at[k, index], device)

    first_side = 4 - 8 * ((z // 4 + lead_slot) % 2)

    def send_far(k, index):
        return remote(mine.at[k, part(index)], far.at[k, part(index)], far_send.at[k, index], far_recv.at[k, index],
                      along(first_side if k == 0 else -first_side))

    def send_across(index):
        return remote(mine.at[2, part(index)], across.at[part(index)], across_send.at[index], across_recv.at[index],
                      along(0, True))

    def send_fresh(slot, half, k):
        return remote(fresh.at[slot, half], fresh.at[slot, half], fresh_send.at[half, k], fresh_recv.at[slot, half],
                      along(sign * MEMBERS[k]))

    loads[0].wait()
    loads[1].wait()
    items = [order_here[0, (offset_here[0] + slot) % 4] for slot in range(2)]
    loads[2].wait()
    for slot in range(2):
        item = items[slot]
        picked = own[0, item // 2]
        turned = jnp.where(item % 2 == 0, picked, picked.T)
        top, bottom = (
            lax.dot_general(a, b, (((1,), (1,)), ((), ())), preferred_element_type=jnp.float32)
            for a, b in ((turned[:256], turned), (turned[256:], turned[256:])))

        def keep(h, first, rows):
            stat[slot, h, first:first + rows.shape[0], :] = rows
            sent[slot, h, first:first + rows.shape[0], :] = rows.astype(jnp.bfloat16)

        pack(top, bottom, keep)
        if slot == 0:
            pl.semaphore_wait(barrier, len(greeted))
        for k in range(3):
            @pl.when(role[slot] == k + 1)
            def _():
                for index in range(len(PARTS)):
                    send_near(slot, k, index).start()
                    send_near(slot, k + 3, index).start()

        @pl.when(role[slot] == 0)
        def _():
            for index in range(len(PARTS)):
                send_near(slot, 6, index).start()

    for step in (2, -2):
        signal(four_ready, along(step))
    signal(peers_ready, peer(1, 0, 0))
    grad_sq = total_square(own[0, 0].astype(jnp.float32)) + total_square(own[0, 1].astype(jnp.float32))
    pl.semaphore_wait(four_ready, 2)

    @pl.when(leads)
    def _():
        for index in range(len(PARTS)):
            for k in range(7):
                send_near(0, k, index).wait_recv()
            total = stat[lead_slot, line, part(index)]
            for k in range(7):
                total += near[k, part(index)].astype(jnp.float32)
            both[line, part(index)] = total
            mine[0, part(index)] = total.astype(jnp.bfloat16)
            send_far(0, index).start()
        for k in range(2):
            for index in range(len(PARTS)):
                send_far(k, index).wait_recv()
                total = both[line, part(index)] + far[k, part(index)].astype(jnp.float32)
                both[line, part(index)] = total
                mine[k + 1, part(index)] = total.astype(jnp.bfloat16)
                (send_far(1, index) if k == 0 else send_across(index)).start()
        for index in range(len(PARTS)):
            send_across(index).wait_recv()
            both[1 - line, part(index)] = across[part(index)].astype(jnp.float32)
        unpack(both, full)
        panels = inverse_root(full[...])
        top, bottom = next(panels), None

        def keep(h, first, rows):
            fresh[lead_slot, h, first:first + rows.shape[0], :] = rows.astype(jnp.bfloat16)

        for half in range(2):
            bottom = next(panels) if half else None
            pack(top, bottom, keep, (half,))
            for k in range(3):
                send_fresh(lead_slot, half, k).start()

    loads[3].wait()
    for slot in range(2):
        @pl.when(role[slot] != 0)
        def _():
            for half in range(2):
                send_fresh(slot, half, 0).wait_recv()
        unpack(fresh.at[slot], roots.at[4 + slot])

    pre_sq = jnp.zeros((1, 1), jnp.float32)
    unscaled = []
    for b in range(2):
        left, right = (
            roots[jnp.where(items[0] == k, 4, jnp.where(items[1] == k, 5, k))] for k in (2 * b, 2 * b + 1))
        done = jnp.dot(left, own[0, b], preferred_element_type=jnp.float32).astype(jnp.bfloat16)
        unscaled.append(jnp.dot(done, right, preferred_element_type=jnp.float32))
        pre_sq += total_square(unscaled[b])

    norms[mp] = jnp.where(positions(8, T)[0] == 0, grad_sq, pre_sq)

    def send_norm(k):
        return remote(norms.at[mp], norms.at[mp], norm_send.at[k], norm_recv.at[mp], peer(*NORM_PEERS[k]))

    def recv_norm(k):
        device = peer(*NORM_PEERS[k])
        return remote(norms.at[device[1]], norms.at[device[1]], norm_send.at[k], norm_recv.at[device[1]], device)

    pl.semaphore_wait(peers_ready, 1)
    for k in range(PEERS - 1):
        send_norm(k).start()
    for k in range(PEERS - 1):
        recv_norm(k).wait_recv()
    total = norms[0]
    for k in range(1, PEERS):
        total += norms[k]
    factor = jnp.sqrt(total[0:1, 0:1] / (total[1:2, 0:1] + 1e-06))
    for b in range(2):
        out[0, b] = (unscaled[b] * factor).astype(jnp.bfloat16)

    for k in range(PEERS - 1):
        send_norm(k).wait_send()
    for index in range(len(PARTS)):
        for slot in range(2):
            @pl.when(role[slot] != 0)
            def _():
                send_near(slot, 0, index).wait_send()
            send_near(slot, 3, index).wait_send()

        @pl.when(leads)
        def _():
            send_across(index).wait_send()
            for k in range(2):
                send_far(k, index).wait_send()
            if index == 0:
                for half in range(2):
                    for k in range(3):
                        send_fresh(lead_slot, half, k).wait_send()


def pinned(array):
    return pltpu.with_memory_space_constraint(array, pltpu.HBM)


def body(grads, order, offset, prev_roots):
    bf16, f32 = jnp.bfloat16, jnp.float32
    dma, parts = pltpu.SemaphoreType.DMA, len(PARTS)
    return pl.pallas_call(
        kernel,
        out_shape=jax.ShapeDtypeStruct((1, 2, N, N), bf16),
        in_specs=[pl.BlockSpec(memory_space=pl.ANY)] * 4,
        out_specs=pl.BlockSpec(memory_space=pltpu.VMEM),
        scratch_shapes=[
            pltpu.SMEM((1, 4), jnp.int32),
            pltpu.SMEM((1,), jnp.int32),
            pltpu.VMEM((1, 2, N, N), bf16),
            pltpu.VMEM((2, 2, HALF, T), f32),
            pltpu.VMEM((2, 2, HALF, T), bf16),
            pltpu.VMEM((7, HALF, T), bf16),
            pltpu.VMEM((3, HALF, T), bf16),
            pltpu.VMEM((2, HALF, T), bf16),
            pltpu.VMEM((HALF, T), bf16),
            pltpu.VMEM((2, HALF, T), f32),
            pltpu.VMEM((2, 2, HALF, T), bf16),
            pltpu.VMEM((N, N), f32),
            pltpu.VMEM((6, N, N), bf16),
            pltpu.VMEM((PEERS, 8, T), f32),
            dma, dma, dma, dma,
            dma((2, 2, parts)), dma((7, parts)),
            dma((2, parts)), dma((2, parts)),
            dma((parts,)), dma((parts,)),
            dma((2, 3)), dma((2, 2)),
            dma((PEERS,)), dma((PEERS,)),
            pltpu.SemaphoreType.REGULAR, pltpu.SemaphoreType.REGULAR,
        ],
        compiler_params=pltpu.CompilerParams(
            collective_id=0, has_side_effects=True, vmem_limit_bytes=40 * 1024 * 1024),
        cost_estimate=pl.CostEstimate(flops=10 * 2 * N ** 3, bytes_accessed=4 * 1024 * 1024, transcendentals=0),
        name="refresh",
    )(pinned(order), offset, pinned(grads), pinned(prev_roots))


def solution(mesh):
    placed = (P("dp", "mp", None, None), P("mp", None), P("mp"), P("mp", None, None))
    return jax.shard_map(
        body, mesh=mesh, in_specs=placed, out_specs=P("dp", "mp", None, None), check_vma=False
    )
```

```python
import jax
import jax.numpy as jnp
from jax import lax
from jax.experimental import pallas as pl
from jax.experimental.pallas import tpu as pltpu
from jax.sharding import PartitionSpec as P

MESH = pl.DeviceIdType.MESH
N = 512
T = 128
REPLICAS = 32
RING = 16
PEERS = 16
RIDGE = 0.1
ABOVE = (((0, 1), (0, 2), (0, 3)), ((1, 2), (1, 3), (2, 3)))
HALF = 4 * T + 16
PARTS = ((0, 208), (208, 176), (384, 144))
MEMBERS = (1, 2, -1)
NORM_PEERS = [(1, 2, 1), (1, 2, 0), (1, 1, 1), (1, 3, 1), (1, 1, 0), (1, 3, 0), (1, 0, 1), (1, 0, 0),
              (0, 2, 1), (0, 2, 0), (0, 1, 1), (0, 3, 1), (0, 1, 0), (0, 3, 0), (0, 0, 1)]


def part(index):
    return pl.ds(*PARTS[index])


def small(a, b):
    return jnp.dot(a.astype(jnp.bfloat16), b.astype(jnp.bfloat16), preferred_element_type=jnp.float32)


def total_square(value):
    return jnp.sum(jnp.sum(value * value, axis=0, keepdims=True), axis=1, keepdims=True)


def positions(rows, columns):
    shape = (rows, columns)
    return lax.broadcasted_iota(jnp.int32, shape, 0), lax.broadcasted_iota(jnp.int32, shape, 1)


def pack(top, bottom, store, halves=(0, 1)):
    row, column = positions(T, T)
    for h in halves:
        tile = lambda i, j: (top[i * T:(i + 1) * T, j * T:(j + 1) * T] if i < 2 else
                             bottom[(i - 2) * T:(i - 1) * T, (j - 2) * T:(j - 1) * T])
        first, second = tile(2 * h, 2 * h), tile(2 * h + 1, 2 * h + 1)
        store(h, 0, jnp.where(column >= row, first, second))
        for index, (i, j) in enumerate(ABOVE[h]):
            store(h, (index + 1) * T, tile(i, j))
        diagonal = jnp.sum(jnp.where(column == row, second, 0.0), axis=0, keepdims=True)
        store(h, 4 * T, jnp.broadcast_to(diagonal, (16, T)))


def unpack(packed, full):
    row, column = positions(T, T)
    for h in range(2):
        both = packed[h, 0:T, :].astype(jnp.float32)
        mirrored = both.T
        diagonal = packed[h, 4 * T:4 * T + 16, :].astype(jnp.float32)[0:1]
        first = jnp.where(column >= row, both, mirrored)
        second = jnp.where(column < row, both, jnp.where(column == row, diagonal, mirrored))
        for block, i in ((first, 2 * h), (second, 2 * h + 1)):
            full[i * T:(i + 1) * T, i * T:(i + 1) * T] = block.astype(full.dtype)
        for index, (i, j) in enumerate(ABOVE[h]):
            block = packed[h, (index + 1) * T:(index + 2) * T, :]
            full[i * T:(i + 1) * T, j * T:(j + 1) * T] = block
            full[j * T:(j + 1) * T, i * T:(i + 1) * T] = block.T


def next_state(a, square=None):
    e2 = ((small(a, a) if square is None else square) - 10.0 * a) * 0.0625
    e4 = 3.125 * e2 + small(e2, e2)
    return 2.44140625 * a + small(e4, a)


def inverse_root(stat):
    row, column = positions(N, N)
    eye = jnp.where(row == column, 1.0, 0.0)
    ridged = stat * (1.0 / (N * REPLICAS)) + RIDGE * eye
    square = small(ridged, ridged)
    start = 2.5 / jnp.sqrt(total_square(ridged))
    a = start * ridged
    b = next_state(a, (start * start) * square)
    c = next_state(b)
    g = small(a, b) * 0.0625 - 0.3125 * (a + b)
    scale = jnp.sqrt(jnp.sqrt(start))
    for rows, columns in ((slice(0, 256), slice(0, N)), (slice(256, N), slice(256, N))):
        yield scale * (1.953125 * eye[rows, columns] + 1.25 * g[rows, columns] - 0.390625 * c[rows, columns]
                       - 0.25 * small(g[rows], c[:, columns]))


def kernel(order, offset, grads, prev, out, order_here, offset_here, own, stat, sent, near, mine, far, across, both, fresh,
           full, roots, norms, order_sem, offset_sem, own_sem, old_sem, near_send, near_recv, far_send, far_recv, across_send,
           across_recv, fresh_send, fresh_recv, norm_send, norm_recv, four_ready, peers_ready):
    dp, mp = lax.axis_index("dp"), lax.axis_index("mp")
    z, line, core = dp // 2, dp % 2, mp % 2
    sign = 1 - 2 * core

    loads = [pltpu.make_async_copy(*refs) for refs in (
        (order, order_here, order_sem), (offset, offset_here, offset_sem), (grads, own, own_sem), (prev, roots.at[pl.ds(0, 4)], old_sem))]
    for load in loads[:3]:
        load.start()

    def along(step, flip=False):
        there = lax.rem(dp + 2 * step + 2 * RING, 2 * RING)
        return (there + 1 - 2 * line if flip else there, mp)

    def peer(y_step, x_step, core_step):
        return (dp, (1 - mp // 8 if y_step else mp // 8) * 8 + (mp // 2 + x_step) % 4 * 2 + (1 - core if core_step else core))

    def signal(semaphore, device):
        pl.semaphore_signal(semaphore, inc=1, device_id=device, device_id_type=MESH)

    barrier = pltpu.get_barrier_semaphore()
    greeted = [along(step) for step in (2, -2, 1, -1)] + [along(step, True) for step in (2, -2, 1, -1, 0)]
    greeted += [peer(1, 0, 0)] + [peer(*steps) for steps in NORM_PEERS if not steps[0]]
    for device in greeted:
        signal(barrier, device)

    role = [(sign * (z - 2 * slot - core) + 2 * RING) % 4 for slot in range(2)]
    leads = jnp.logical_or(role[0] == 0, role[1] == 0)
    lead_slot = jnp.where(role[1] == 0, 1, 0)

    def remote(source, target, send_sem, recv_sem, device):
        return pltpu.make_async_remote_copy(
            src_ref=source, dst_ref=target, send_sem=send_sem, recv_sem=recv_sem, device_id=device, device_id_type=MESH)

    def send_near(slot, k, index):
        half = line if k < 3 else 1 - line
        device = along(0 if k == 6 else -sign * MEMBERS[k % 3], k >= 3)
        return remote(sent.at[slot, half, part(index)], near.at[k, part(index)],
                      near_send.at[slot, 0 if k < 3 else 1, index], near_recv.at[k, index], device)

    first_side = 4 - 8 * ((z // 4 + lead_slot) % 2)

    def send_far(k, index):
        return remote(mine.at[k, part(index)], far.at[k, part(index)], far_send.at[k, index], far_recv.at[k, index],
                      along(first_side if k == 0 else -first_side))

    def send_across(index):
        return remote(mine.at[2, part(index)], across.at[part(index)], across_send.at[index], across_recv.at[index],
                      along(0, True))

    def send_fresh(slot, half, k):
        return remote(fresh.at[slot, half], fresh.at[slot, half], fresh_send.at[half, k], fresh_recv.at[slot, half],
                      along(sign * MEMBERS[k]))

    loads[0].wait()
    loads[1].wait()
    items = [order_here[0, (offset_here[0] + slot) % 4] for slot in range(2)]
    loads[2].wait()
    loads[3].start()
    for slot in range(2):
        item = items[slot]
        picked = own[0, item // 2]
        turned = jnp.where(item % 2 == 0, picked, picked.T)
        top, bottom = (
            lax.dot_general(a, b, (((1,), (1,)), ((), ())), preferred_element_type=jnp.float32)
            for a, b in ((turned[:256], turned), (turned[256:], turned[256:])))

        def keep(h, first, rows):
            stat[slot, h, first:first + rows.shape[0], :] = rows
            sent[slot, h, first:first + rows.shape[0], :] = rows.astype(jnp.bfloat16)

        pack(top, bottom, keep)
        if slot == 0:
            pl.semaphore_wait(barrier, len(greeted))
        for k in range(3):
            @pl.when(role[slot] == k + 1)
            def _():
                for index in range(len(PARTS)):
                    send_near(slot, k, index).start()
                    send_near(slot, k + 3, index).start()

        @pl.when(role[slot] == 0)
        def _():
            for index in range(len(PARTS)):
                send_near(slot, 6, index).start()

    for step in (2, -2):
        signal(four_ready, along(step))
    signal(peers_ready, peer(1, 0, 0))
    grad_sq = total_square(own[0, 0].astype(jnp.float32)) + total_square(own[0, 1].astype(jnp.float32))
    pl.semaphore_wait(four_ready, 2)

    @pl.when(leads)
    def _():
        for index in range(len(PARTS)):
            for k in range(7):
                send_near(0, k, index).wait_recv()
            total = stat[lead_slot, line, part(index)]
            for k in range(7):
                total += near[k, part(index)].astype(jnp.float32)
            both[line, part(index)] = total
            mine[0, part(index)] = total.astype(jnp.bfloat16)
            send_far(0, index).start()
        for k in range(2):
            for index in range(len(PARTS)):
                send_far(k, index).wait_recv()
                total = both[line, part(index)] + far[k, part(index)].astype(jnp.float32)
                both[line, part(index)] = total
                mine[k + 1, part(index)] = total.astype(jnp.bfloat16)
                (send_far(1, index) if k == 0 else send_across(index)).start()
        for index in range(len(PARTS)):
            send_across(index).wait_recv()
            both[1 - line, part(index)] = across[part(index)].astype(jnp.float32)
        unpack(both, full)
        panels = inverse_root(full[...])
        top, bottom = next(panels), None

        def keep(h, first, rows):
            fresh[lead_slot, h, first:first + rows.shape[0], :] = rows.astype(jnp.bfloat16)

        for half in range(2):
            bottom = next(panels) if half else None
            pack(top, bottom, keep, (half,))
            for k in (1, 2, 0):
                send_fresh(lead_slot, half, k).start()

    loads[3].wait()
    for slot in range(2):
        @pl.when(role[slot] != 0)
        def _():
            for half in range(2):
                send_fresh(slot, half, 0).wait_recv()
        unpack(fresh.at[slot], roots.at[4 + slot])

    pre_sq = jnp.zeros((1, 1), jnp.float32)
    unscaled = []
    for b in range(2):
        left, right = (
            roots[jnp.where(items[0] == k, 4, jnp.where(items[1] == k, 5, k))] for k in (2 * b, 2 * b + 1))
        done = jnp.dot(left, own[0, b], preferred_element_type=jnp.float32).astype(jnp.bfloat16)
        unscaled.append(jnp.dot(done, right, preferred_element_type=jnp.float32))
        pre_sq += total_square(unscaled[b])

    norms[mp] = jnp.where(positions(8, T)[0] == 0, grad_sq, pre_sq)

    def send_norm(k):
        return remote(norms.at[mp], norms.at[mp], norm_send.at[k], norm_recv.at[mp], peer(*NORM_PEERS[k]))

    def recv_norm(k):
        device = peer(*NORM_PEERS[k])
        return remote(norms.at[device[1]], norms.at[device[1]], norm_send.at[k], norm_recv.at[device[1]], device)

    pl.semaphore_wait(peers_ready, 1)
    for k in range(PEERS - 1):
        send_norm(k).start()
    for k in range(PEERS - 1):
        recv_norm(k).wait_recv()
    total = norms[0]
    for k in range(1, PEERS):
        total += norms[k]
    factor = jnp.sqrt(total[0:1, 0:1] / (total[1:2, 0:1] + 1e-06))
    for b in range(2):
        out[0, b] = (unscaled[b] * factor).astype(jnp.bfloat16)

    for k in range(PEERS - 1):
        send_norm(k).wait_send()
    for index in range(len(PARTS)):
        for slot in range(2):
            @pl.when(role[slot] != 0)
            def _():
                send_near(slot, 0, index).wait_send()
            send_near(slot, 3, index).wait_send()

        @pl.when(leads)
        def _():
            send_across(index).wait_send()
            for k in range(2):
                send_far(k, index).wait_send()
            if index == 0:
                for half in range(2):
                    for k in range(3):
                        send_fresh(lead_slot, half, k).wait_send()


def pinned(array):
    return pltpu.with_memory_space_constraint(array, pltpu.HBM)


def body(grads, order, offset, prev_roots):
    bf16, f32 = jnp.bfloat16, jnp.float32
    dma, parts = pltpu.SemaphoreType.DMA, len(PARTS)
    return pl.pallas_call(
        kernel,
        out_shape=jax.ShapeDtypeStruct((1, 2, N, N), bf16),
        in_specs=[pl.BlockSpec(memory_space=pl.ANY)] * 4,
        out_specs=pl.BlockSpec(memory_space=pltpu.VMEM),
        scratch_shapes=[
            pltpu.SMEM((1, 4), jnp.int32),
            pltpu.SMEM((1,), jnp.int32),
            pltpu.VMEM((1, 2, N, N), bf16),
            pltpu.VMEM((2, 2, HALF, T), f32),
            pltpu.VMEM((2, 2, HALF, T), bf16),
            pltpu.VMEM((7, HALF, T), bf16),
            pltpu.VMEM((3, HALF, T), bf16),
            pltpu.VMEM((2, HALF, T), bf16),
            pltpu.VMEM((HALF, T), bf16),
            pltpu.VMEM((2, HALF, T), f32),
            pltpu.VMEM((2, 2, HALF, T), bf16),
            pltpu.VMEM((N, N), f32),
            pltpu.VMEM((6, N, N), bf16),
            pltpu.VMEM((PEERS, 8, T), f32),
            dma, dma, dma, dma,
            dma((2, 2, parts)), dma((7, parts)),
            dma((2, parts)), dma((2, parts)),
            dma((parts,)), dma((parts,)),
            dma((2, 3)), dma((2, 2)),
            dma((PEERS,)), dma((PEERS,)),
            pltpu.SemaphoreType.REGULAR, pltpu.SemaphoreType.REGULAR,
        ],
        compiler_params=pltpu.CompilerParams(
            collective_id=0, has_side_effects=True, vmem_limit_bytes=40 * 1024 * 1024),
        cost_estimate=pl.CostEstimate(flops=10 * 2 * N ** 3, bytes_accessed=4 * 1024 * 1024, transcendentals=0),
        name="refresh",
    )(pinned(order), offset, pinned(grads), pinned(prev_roots))


def solution(mesh):
    placed = (P("dp", "mp", None, None), P("mp", None), P("mp"), P("mp", None, None))
    return jax.shard_map(
        body, mesh=mesh, in_specs=placed, out_specs=P("dp", "mp", None, None), check_vma=False
    )
```

```python
import jax
import jax.numpy as jnp
from jax import lax
from jax.experimental import pallas as pl
from jax.experimental.pallas import tpu as pltpu
from jax.sharding import PartitionSpec as P

MESH = pl.DeviceIdType.MESH
N = 512
T = 128
REPLICAS = 32
RING = 16
PEERS = 16
RIDGE = 0.1
ABOVE = (((0, 1), (0, 2), (0, 3)), ((1, 2), (1, 3), (2, 3)))
HALF = 4 * T + 16
PARTS = ((0, 208), (208, 176), (384, 144))
MEMBERS = (1, 2, -1)
NORM_PEERS = [(1, 2, 1), (1, 2, 0), (1, 1, 1), (1, 3, 1), (1, 1, 0), (1, 3, 0), (1, 0, 1), (1, 0, 0),
              (0, 2, 1), (0, 2, 0), (0, 1, 1), (0, 3, 1), (0, 1, 0), (0, 3, 0), (0, 0, 1)]


def part(index):
    return pl.ds(*PARTS[index])


def small(a, b):
    return jnp.dot(a.astype(jnp.bfloat16), b.astype(jnp.bfloat16), preferred_element_type=jnp.float32)


def total_square(value):
    return jnp.sum(jnp.sum(value * value, axis=0, keepdims=True), axis=1, keepdims=True)


def positions(rows, columns):
    shape = (rows, columns)
    return lax.broadcasted_iota(jnp.int32, shape, 0), lax.broadcasted_iota(jnp.int32, shape, 1)


def pack(top, bottom, store, halves=(0, 1)):
    row, column = positions(T, T)
    for h in halves:
        tile = lambda i, j: (top[i * T:(i + 1) * T, j * T:(j + 1) * T] if i < 2 else
                             bottom[(i - 2) * T:(i - 1) * T, (j - 2) * T:(j - 1) * T])
        first, second = tile(2 * h, 2 * h), tile(2 * h + 1, 2 * h + 1)
        store(h, 0, jnp.where(column >= row, first, second))
        for index, (i, j) in enumerate(ABOVE[h]):
            store(h, (index + 1) * T, tile(i, j))
        diagonal = jnp.sum(jnp.where(column == row, second, 0.0), axis=0, keepdims=True)
        store(h, 4 * T, jnp.broadcast_to(diagonal, (16, T)))


def unpack(packed, full):
    row, column = positions(T, T)
    for h in range(2):
        both = packed[h, 0:T, :].astype(jnp.float32)
        mirrored = both.T
        diagonal = packed[h, 4 * T:4 * T + 16, :].astype(jnp.float32)[0:1]
        first = jnp.where(column >= row, both, mirrored)
        second = jnp.where(column < row, both, jnp.where(column == row, diagonal, mirrored))
        for block, i in ((first, 2 * h), (second, 2 * h + 1)):
            full[i * T:(i + 1) * T, i * T:(i + 1) * T] = block.astype(full.dtype)
        for index, (i, j) in enumerate(ABOVE[h]):
            block = packed[h, (index + 1) * T:(index + 2) * T, :]
            full[i * T:(i + 1) * T, j * T:(j + 1) * T] = block
            full[j * T:(j + 1) * T, i * T:(i + 1) * T] = block.T


def next_state(a, square=None):
    e2 = ((small(a, a) if square is None else square) - 10.0 * a) * 0.0625
    e4 = 3.125 * e2 + small(e2, e2)
    return lambda rows: 2.44140625 * a[rows] + small(e4[rows], a)


def inverse_root(stat):
    row, column = positions(N, N)
    eye = jnp.where(row == column, 1.0, 0.0)
    ridged = stat * (1.0 / (N * REPLICAS)) + RIDGE * eye
    square = small(ridged, ridged)
    start = 2.5 / jnp.sqrt(total_square(ridged))
    a = start * ridged
    b = next_state(a, (start * start) * square)(slice(0, N))
    c_rows = next_state(b)
    g = small(a, b) * 0.0625 - 0.3125 * (a + b)
    scale = jnp.sqrt(jnp.sqrt(start))
    for rows, columns in ((slice(0, 256), slice(0, N)), (slice(256, N), slice(256, N))):
        c = c_rows(rows)
        yield scale * (1.953125 * eye[rows, columns] + 1.25 * g[rows, columns] - 0.390625 * c[:, columns]
                       - 0.25 * small(c, g[:, columns]))


def kernel(order, offset, grads, prev, out, order_here, offset_here, own, stat, sent, near, mine, far, across, both, fresh,
           full, roots, norms, order_sem, offset_sem, own_sem, old_sem, near_send, near_recv, far_send, far_recv, across_send,
           across_recv, fresh_send, fresh_recv, norm_send, norm_recv, four_ready, peers_ready):
    dp, mp = lax.axis_index("dp"), lax.axis_index("mp")
    z, line, core = dp // 2, dp % 2, mp % 2
    sign = 1 - 2 * core

    loads = [pltpu.make_async_copy(*refs) for refs in (
        (order, order_here, order_sem), (offset, offset_here, offset_sem), (grads, own, own_sem), (prev, roots.at[pl.ds(0, 4)], old_sem))]
    for load in loads[:3]:
        load.start()

    def along(step, flip=False):
        there = lax.rem(dp + 2 * step + 2 * RING, 2 * RING)
        return (there + 1 - 2 * line if flip else there, mp)

    def peer(y_step, x_step, core_step):
        return (dp, (1 - mp // 8 if y_step else mp // 8) * 8 + (mp // 2 + x_step) % 4 * 2 + (1 - core if core_step else core))

    def signal(semaphore, device):
        pl.semaphore_signal(semaphore, inc=1, device_id=device, device_id_type=MESH)

    barrier = pltpu.get_barrier_semaphore()
    greeted = [along(step) for step in (2, -2, 1, -1)] + [along(step, True) for step in (2, -2, 1, -1, 0)]
    greeted += [peer(1, 0, 0)] + [peer(*steps) for steps in NORM_PEERS if not steps[0]]
    for device in greeted:
        signal(barrier, device)

    role = [(sign * (z - 2 * slot - core) + 2 * RING) % 4 for slot in range(2)]
    leads = jnp.logical_or(role[0] == 0, role[1] == 0)
    lead_slot = jnp.where(role[1] == 0, 1, 0)

    def remote(source, target, send_sem, recv_sem, device):
        return pltpu.make_async_remote_copy(
            src_ref=source, dst_ref=target, send_sem=send_sem, recv_sem=recv_sem, device_id=device, device_id_type=MESH)

    def send_near(slot, k, index):
        half = line if k < 3 else 1 - line
        device = along(0 if k == 6 else -sign * MEMBERS[k % 3], k >= 3)
        return remote(sent.at[slot, half, part(index)], near.at[k, part(index)],
                      near_send.at[slot, 0 if k < 3 else 1, index], near_recv.at[k, index], device)

    first_side = 4 - 8 * ((z // 4 + lead_slot) % 2)

    def send_far(k, index):
        return remote(mine.at[k, part(index)], far.at[k, part(index)], far_send.at[k, index], far_recv.at[k, index],
                      along(first_side if k == 0 else -first_side))

    def send_across(index):
        return remote(mine.at[2, part(index)], across.at[part(index)], across_send.at[index], across_recv.at[index],
                      along(0, True))

    def send_fresh(slot, half, k):
        return remote(fresh.at[slot, half], fresh.at[slot, half], fresh_send.at[half, k], fresh_recv.at[slot, half],
                      along(sign * MEMBERS[k]))

    loads[0].wait()
    loads[1].wait()
    items = [order_here[0, (offset_here[0] + slot) % 4] for slot in range(2)]
    loads[2].wait()
    loads[3].start()
    for slot in range(2):
        item = items[slot]
        picked = own[0, item // 2]
        turned = jnp.where(item % 2 == 0, picked, picked.T)
        top, bottom = (
            lax.dot_general(a, b, (((1,), (1,)), ((), ())), preferred_element_type=jnp.float32)
            for a, b in ((turned[:256], turned), (turned[256:], turned[256:])))

        def keep(h, first, rows):
            stat[slot, h, first:first + rows.shape[0], :] = rows
            sent[slot, h, first:first + rows.shape[0], :] = rows.astype(jnp.bfloat16)

        pack(top, bottom, keep)
        if slot == 0:
            pl.semaphore_wait(barrier, len(greeted))
        for k in range(3):
            @pl.when(role[slot] == k + 1)
            def _():
                for index in range(len(PARTS)):
                    send_near(slot, k, index).start()
                    send_near(slot, k + 3, index).start()

        @pl.when(role[slot] == 0)
        def _():
            for index in range(len(PARTS)):
                send_near(slot, 6, index).start()

    for step in (2, -2):
        signal(four_ready, along(step))
    signal(peers_ready, peer(1, 0, 0))
    grad_sq = total_square(own[0, 0].astype(jnp.float32)) + total_square(own[0, 1].astype(jnp.float32))
    pl.semaphore_wait(four_ready, 2)

    @pl.when(leads)
    def _():
        for index in range(len(PARTS)):
            for k in range(7):
                send_near(0, k, index).wait_recv()
            total = stat[lead_slot, line, part(index)]
            for k in range(7):
                total += near[k, part(index)].astype(jnp.float32)
            both[line, part(index)] = total
            mine[0, part(index)] = total.astype(jnp.bfloat16)
            send_far(0, index).start()
        for k in range(2):
            for index in range(len(PARTS)):
                send_far(k, index).wait_recv()
                total = both[line, part(index)] + far[k, part(index)].astype(jnp.float32)
                both[line, part(index)] = total
                mine[k + 1, part(index)] = total.astype(jnp.bfloat16)
                (send_far(1, index) if k == 0 else send_across(index)).start()
        for index in range(len(PARTS)):
            send_across(index).wait_recv()
            both[1 - line, part(index)] = across[part(index)].astype(jnp.float32)
        unpack(both, full)
        panels = inverse_root(full[...])
        top, bottom = next(panels), None

        def keep(h, first, rows):
            fresh[lead_slot, h, first:first + rows.shape[0], :] = rows.astype(jnp.bfloat16)

        for half in range(2):
            bottom = next(panels) if half else None
            pack(top, bottom, keep, (half,))
            for k in (1, 2, 0):
                send_fresh(lead_slot, half, k).start()

    loads[3].wait()
    for slot in range(2):
        @pl.when(role[slot] != 0)
        def _():
            for half in range(2):
                send_fresh(slot, half, 0).wait_recv()
        unpack(fresh.at[slot], roots.at[4 + slot])

    pre_sq = jnp.zeros((1, 1), jnp.float32)
    unscaled = []
    for b in range(2):
        left, right = (
            roots[jnp.where(items[0] == k, 4, jnp.where(items[1] == k, 5, k))] for k in (2 * b, 2 * b + 1))
        done = jnp.dot(left, own[0, b], preferred_element_type=jnp.float32).astype(jnp.bfloat16)
        unscaled.append(jnp.dot(done, right, preferred_element_type=jnp.float32))
        pre_sq += total_square(unscaled[b])

    norms[mp] = jnp.where(positions(8, T)[0] == 0, grad_sq, pre_sq)

    def send_norm(k):
        return remote(norms.at[mp], norms.at[mp], norm_send.at[k], norm_recv.at[mp], peer(*NORM_PEERS[k]))

    def recv_norm(k):
        device = peer(*NORM_PEERS[k])
        return remote(norms.at[device[1]], norms.at[device[1]], norm_send.at[k], norm_recv.at[device[1]], device)

    pl.semaphore_wait(peers_ready, 1)
    for k in range(PEERS - 1):
        send_norm(k).start()
    for k in range(PEERS - 1):
        recv_norm(k).wait_recv()
    total = norms[0]
    for k in range(1, PEERS):
        total += norms[k]
    factor = jnp.sqrt(total[0:1, 0:1] / (total[1:2, 0:1] + 1e-06))
    for b in range(2):
        out[0, b] = (unscaled[b] * factor).astype(jnp.bfloat16)

    for k in range(PEERS - 1):
        send_norm(k).wait_send()
    for index in range(len(PARTS)):
        for slot in range(2):
            @pl.when(role[slot] != 0)
            def _():
                send_near(slot, 0, index).wait_send()
            send_near(slot, 3, index).wait_send()

        @pl.when(leads)
        def _():
            send_across(index).wait_send()
            for k in range(2):
                send_far(k, index).wait_send()
            if index == 0:
                for half in range(2):
                    for k in range(3):
                        send_fresh(lead_slot, half, k).wait_send()


def pinned(array):
    return pltpu.with_memory_space_constraint(array, pltpu.HBM)


def body(grads, order, offset, prev_roots):
    bf16, f32 = jnp.bfloat16, jnp.float32
    dma, parts = pltpu.SemaphoreType.DMA, len(PARTS)
    return pl.pallas_call(
        kernel,
        out_shape=jax.ShapeDtypeStruct((1, 2, N, N), bf16),
        in_specs=[pl.BlockSpec(memory_space=pl.ANY)] * 4,
        out_specs=pl.BlockSpec(memory_space=pltpu.VMEM),
        scratch_shapes=[
            pltpu.SMEM((1, 4), jnp.int32),
            pltpu.SMEM((1,), jnp.int32),
            pltpu.VMEM((1, 2, N, N), bf16),
            pltpu.VMEM((2, 2, HALF, T), f32),
            pltpu.VMEM((2, 2, HALF, T), bf16),
            pltpu.VMEM((7, HALF, T), bf16),
            pltpu.VMEM((3, HALF, T), bf16),
            pltpu.VMEM((2, HALF, T), bf16),
            pltpu.VMEM((HALF, T), bf16),
            pltpu.VMEM((2, HALF, T), f32),
            pltpu.VMEM((2, 2, HALF, T), bf16),
            pltpu.VMEM((N, N), f32),
            pltpu.VMEM((6, N, N), bf16),
            pltpu.VMEM((PEERS, 8, T), f32),
            dma, dma, dma, dma,
            dma((2, 2, parts)), dma((7, parts)),
            dma((2, parts)), dma((2, parts)),
            dma((parts,)), dma((parts,)),
            dma((2, 3)), dma((2, 2)),
            dma((PEERS,)), dma((PEERS,)),
            pltpu.SemaphoreType.REGULAR, pltpu.SemaphoreType.REGULAR,
        ],
        compiler_params=pltpu.CompilerParams(
            collective_id=0, has_side_effects=True, vmem_limit_bytes=40 * 1024 * 1024),
        cost_estimate=pl.CostEstimate(flops=10 * 2 * N ** 3, bytes_accessed=4 * 1024 * 1024, transcendentals=0),
        name="refresh",
    )(pinned(order), offset, pinned(grads), pinned(prev_roots))


def solution(mesh):
    placed = (P("dp", "mp", None, None), P("mp", None), P("mp"), P("mp", None, None))
    return jax.shard_map(
        body, mesh=mesh, in_specs=placed, out_specs=P("dp", "mp", None, None), check_vma=False
    )
```
